256 devices in a mesh: row: 16 (over z_hi, x, core), col: 16 (over z_lo, y).
Axes of the slice: x: 4, y: 4, z: 8 (z_hi: 2, z_lo: 4; z = z_hi * 4 + z_lo), core: 2. Of those that a mesh axis runs over, the one named last changes fastest.
Arguments:
- upper_vals: bfloat16 [512, 6, 128, 128], P(('row', 'col')), may hold values from -1 to 1
- upper_cols: int32 [512, 6], P(('row', 'col')), may hold values from 0 to 511, as said below
- result_cols: int32 [512, 8], P(('row', 'col')), may hold values from 0 to 511, as said below
Outputs:
- result_blocks: bfloat16 [512, 8, 128, 128], P(('row', 'col'))
The draws below stay inside these ranges and needn't reach their ends.
Inputs may be any that keep to these rules, and one draw needn't show every extreme that they name: `upper_cols`: slot 0 of block row I holds I; its other slots hold 5 distinct columns (I + k) mod 512 with 1 <= k <= 7. `result_cols`: block row I holds 8 distinct columns (I + k) mod 512 with 1 <= k <= 14.
All inputs are finite; a program needn't handle non-finite values.
Results may differ from the reference program's by a relative error of at most 0.0035.
Values may be sent and summed in bfloat16 or wider, within the bound.
A program may use at most 64 MiB of HBM per device.

```python
import jax
import jax.numpy as jnp
from jax import lax

BLK = 128
W = 7
SU = 6
SR = 8
ROWS_DEV = 2
NBLK = 512


def offsets_from_key(key, choice_count, keep_count):
    scores = jax.random.randint(key, (NBLK, choice_count), 0, 1 << 20) * choice_count + jnp.arange(choice_count, dtype=jnp.int32)[None, :]
    ranking = jnp.argsort(scores, axis=1)
    return ranking[:, :keep_count].astype(jnp.int32) + 1


def draw_upper_cols(key, part):
    extra_steps = offsets_from_key(jax.random.fold_in(key, 11), W, SU - 1)
    all_steps = jnp.concatenate([jnp.zeros((NBLK, 1), jnp.int32), extra_steps], axis=1)
    return (jnp.arange(NBLK, dtype=jnp.int32)[:, None] + all_steps) % NBLK


def draw_result_cols(key, part):
    all_steps = offsets_from_key(jax.random.fold_in(key, 23), 2 * W, SR)
    return (jnp.arange(NBLK, dtype=jnp.int32)[:, None] + all_steps) % NBLK


def levels(rng, shape, pieces, smallest, largest):
    level, own = 1.0, jax.random.fold_in(rng, 6)
    for dim, parts in pieces:
        heights = jnp.exp(jax.random.uniform(jax.random.fold_in(own, dim), (parts,), jnp.float32, smallest / len(pieces), largest / len(pieces)))
        level = level * jnp.repeat(heights, shape[dim] // parts).reshape([-1 if axis == dim else 1 for axis in range(len(shape))])
    return level


def bell_draw(stream_key, shape, deviation, most, shards=(), held_as=jnp.bfloat16):
    gain = levels(stream_key, shape, shards, -0.22, 0.18) if shards else 1.0
    drawn = jax.random.normal(stream_key, shape, jnp.float32) * deviation * gain
    return jnp.minimum(jnp.maximum(drawn, -most), most).astype(held_as)


def setup_inputs(seed: int = 0) -> dict:
    keys = jax.random.split(jax.random.key(seed), 4)
    return {
        "upper_vals": bell_draw(keys[0], (NBLK, SU, BLK, BLK), 32 ** -0.5, 1.0, ((0, 256),)),
        "upper_cols": draw_upper_cols(jax.random.fold_in(keys[3], 71), 0),
        "result_cols": draw_result_cols(jax.random.fold_in(keys[3], 71), 0),
    }


def band_rows(upper_win, offset_win, band_reach):
    row_total = upper_win.shape[0] - band_reach
    select = (offset_win[:, :, None] == jnp.arange(band_reach + 1, dtype=jnp.int32)[None, None, :]).astype(jnp.float32)
    packed = jnp.einsum("nso,nsab->noab", select, upper_win.astype(jnp.float32)).astype(jnp.bfloat16)
    own_rows = packed[band_reach:]
    diagonal = own_rows[:, 0].astype(jnp.float32)
    diagonal = (diagonal + jnp.swapaxes(diagonal, -1, -2)).astype(jnp.bfloat16)
    lower_part = [jnp.swapaxes(packed[band_reach - shift_by: band_reach - shift_by + row_total, shift_by], -1, -2) for shift_by in range(band_reach, 0, -1)]
    return jnp.concatenate([jnp.stack(lower_part, axis=1), diagonal[:, None], own_rows[:, 1:]], axis=1)


def row_products(band_window, row_index, step_offsets, band_reach):
    band_width = 2 * band_reach + 1
    flat_band = band_window.reshape((-1,) + band_window.shape[2:])
    position = jnp.arange(band_width, dtype=jnp.int32)
    source = position[None, :] - step_offsets[:, None]
    flat_index = (row_index + step_offsets)[:, None] * band_width + jnp.maximum(source, 0)
    partner = jnp.take(flat_band, flat_index, axis=0)
    partner = jnp.where((source >= 0)[:, :, None, None], partner, jnp.zeros_like(partner))
    own_row = lax.dynamic_index_in_dim(band_window, row_index, 0, keepdims=False)
    return jnp.einsum("eac,tebc->tab", own_row.astype(jnp.float32), partner.astype(jnp.float32))


def reference(upper_vals, upper_cols, result_cols):
    block_total = upper_vals.shape[0]
    row_count = ROWS_DEV
    all_ids = jnp.arange(block_total, dtype=jnp.int32)
    offsets = (upper_cols - all_ids[:, None]) % block_total
    step_all = (result_cols - all_ids[:, None]) % block_total

    def one_group(group):
        first_row = group * row_count
        window_ids = (first_row - W + jnp.arange(row_count + 3 * W, dtype=jnp.int32)) % block_total
        upper_win = jnp.take(upper_vals, window_ids, axis=0)
        offset_win = jnp.take(offsets, window_ids, axis=0)
        band_window = band_rows(upper_win, offset_win, W)
        steps_here = lax.dynamic_slice_in_dim(step_all, first_row, row_count, 0)

        def one_row(row_index):
            return row_products(band_window, row_index, steps_here[row_index], W).astype(jnp.bfloat16)

        return lax.map(one_row, jnp.arange(row_count, dtype=jnp.int32))

    grouped = lax.map(one_group, jnp.arange(block_total // row_count, dtype=jnp.int32))
    return grouped.reshape((block_total,) + grouped.shape[2:])
```

```python
import jax
import jax.numpy as jnp
from jax import lax
from jax.experimental import pallas as pl
from jax.experimental.pallas import tpu as pltpu
from jax.sharding import PartitionSpec as P

BLK = 128
REACH = 7
SLOTS = 6
NONE = SLOTS
ROWS = 2
STEPS = 2 * REACH
FIRST = REACH - 1
LAST = 2 * REACH
BEHIND = (-3, -2, -1)
AHEAD = (1, 2, 3, 4)
OTHERS = BEHIND + AHEAD
SENT = {
    -3: ((0, 2), (1, 3)),
    -2: ((0, 4), (1, 5)),
    -1: ((0, 5), (1, 5)),
    1: ((0, 6), (1, 6)),
    2: ((0, 6), (1, 6)),
    3: ((0, 6), (1, 6)),
    4: ((0, 6),),
}


def band_kernel(device_total, block_total, vals, cols, kept, out, *scratch):
    held = dict(zip(OTHERS, scratch[:7]))
    places = dict(zip(OTHERS, scratch[7:14]))
    own, own_places, left, right, every, send_sem, recv_sem, psend_sem, precv_sem = scratch[14:]
    inner = lax.axis_size("col")
    me = lax.axis_index("row") * inner + lax.axis_index("col")

    def device(distance):
        there = lax.rem(me + distance + device_total, device_total)
        return (there // inner, lax.rem(there, inner))

    barrier = pltpu.get_barrier_semaphore()
    for m in (-4, -3, -2, -1, 1, 2, 3, 4):
        pl.semaphore_signal(barrier, inc=1, device_id=device(m), device_id_type=pl.DeviceIdType.MESH)

    zero = jnp.zeros((BLK, BLK), jnp.bfloat16)
    for r in range(ROWS):
        offs = [lax.rem(cols[r, s] - (me * ROWS + r) + block_total, block_total) for s in range(SLOTS)]
        ranks = [
            sum((offs[t] > offs[s]).astype(jnp.int32) for t in range(1, SLOTS) if t != s)
            for s in range(1, SLOTS)
        ]
        for j in range(SLOTS - 1):
            slot = sum(s * (ranks[s - 1] == j).astype(jnp.int32) for s in range(1, SLOTS))
            own[r, j] = vals[r, jnp.minimum(slot, SLOTS - 1)]
        own[r, SLOTS - 1] = vals[r, 0]
        own[r, NONE] = zero
        own_places[r, 0] = SLOTS - 1
        for o in range(1, REACH + 1):
            place = NONE
            for s in range(1, SLOTS):
                place = jnp.where(offs[s] == o, ranks[s - 1], place)
            own_places[r, o] = place
    for m in OTHERS:
        for r, _ in SENT[m]:
            held[m][r, NONE] = zero

    pl.semaphore_wait(barrier, 8)

    copies = []
    number = 0
    for k, m in enumerate(OTHERS):
        copy = pltpu.make_async_remote_copy(
            src_ref=own_places,
            dst_ref=places[m],
            send_sem=psend_sem.at[k],
            recv_sem=precv_sem.at[k],
            device_id=device(-m),
            device_id_type=pl.DeviceIdType.MESH,
        )
        copy.start()
        copies.append(copy)
    for m in (1, -1, 2, -2, 3, -3, 4):
        for r, count in SENT[m]:
            copy = pltpu.make_async_remote_copy(
                src_ref=own.at[r, pl.ds(0, count)],
                dst_ref=held[m].at[r, pl.ds(0, count)],
                send_sem=send_sem.at[number],
                recv_sem=recv_sem.at[number],
                device_id=device(-m),
                device_id_type=pl.DeviceIdType.MESH,
            )
            copy.start()
            copies.append(copy)
            number += 1
    for copy in copies:
        copy.wait()

    def stored(row, offset):
        m, r = row // 2 - 3, row % 2
        if m == 0:
            return own[r, own_places[r, offset]]
        return held[m][r, places[m][r, offset]]

    def block(a, b):
        if a == b:
            d = stored(a, 0)
            return (d.astype(jnp.float32) + d.T.astype(jnp.float32)).astype(jnp.bfloat16)
        if abs(a - b) > REACH or min(a, b) > LAST:
            return zero
        if a < b:
            return stored(a, b - a)
        return stored(b, a - b).T

    for a in range(ROWS):
        for k in range(LAST + 2):
            lost = k > LAST or k < a
            left[pl.ds(a * BLK, BLK), pl.ds(k * BLK, BLK)] = zero if lost else block(FIRST + a, k)
    for p in range(REACH + 1):
        for k in range(2 * p, LAST + 2):
            for c in range(2):
                j = FIRST + 1 + 2 * p + c
                right[p, pl.ds(k * BLK, BLK), pl.ds(c * BLK, BLK)] = zero if k > LAST else block(k, j)
    for p in range(REACH + 1):
        deep = pl.ds(2 * p * BLK, (LAST + 2 - 2 * p) * BLK)
        got = jnp.dot(left[:, deep], right[p, deep, :], preferred_element_type=jnp.float32).astype(jnp.bfloat16)
        for a in range(ROWS):
            for c in range(2):
                step = 2 * p + c + 1 - a
                if 1 <= step <= STEPS:
                    every[a, step - 1] = got[a * BLK : (a + 1) * BLK, c * BLK : (c + 1) * BLK]
    for a in range(ROWS):
        for t in range(kept.shape[1]):
            step = lax.rem(kept[a, t] - (me * ROWS + a) + block_total, block_total)
            out[a, t] = every[a, jnp.clip(step - 1, 0, STEPS - 1)]


def on_device(upper_vals, upper_cols, result_cols):
    device_total = lax.axis_size("row") * lax.axis_size("col")
    rows, kept_count = result_cols.shape
    places_shape = pltpu.SMEM((ROWS, REACH + 1), jnp.int32)
    copy_total = sum(len(part) for part in SENT.values())

    def kernel(*refs):
        band_kernel(device_total, device_total * ROWS, *refs)

    return pl.pallas_call(
        kernel,
        out_shape=jax.ShapeDtypeStruct((rows, kept_count, BLK, BLK), jnp.bfloat16),
        in_specs=[
            pl.BlockSpec(memory_space=pltpu.VMEM),
            pl.BlockSpec(memory_space=pltpu.SMEM),
            pl.BlockSpec(memory_space=pltpu.SMEM),
        ],
        out_specs=pl.BlockSpec(memory_space=pltpu.VMEM),
        scratch_shapes=[
            *[pltpu.VMEM((ROWS, SLOTS + 1, BLK, BLK), jnp.bfloat16) for _ in OTHERS],
            *[places_shape for _ in OTHERS],
            pltpu.VMEM((ROWS, SLOTS + 1, BLK, BLK), jnp.bfloat16),
            places_shape,
            pltpu.VMEM((ROWS * BLK, (LAST + 2) * BLK), jnp.bfloat16),
            pltpu.VMEM((REACH + 1, (LAST + 2) * BLK, 2 * BLK), jnp.bfloat16),
            pltpu.VMEM((ROWS, STEPS, BLK, BLK), jnp.bfloat16),
            pltpu.SemaphoreType.DMA((copy_total,)),
            pltpu.SemaphoreType.DMA((copy_total,)),
            pltpu.SemaphoreType.DMA((len(OTHERS),)),
            pltpu.SemaphoreType.DMA((len(OTHERS),)),
        ],
        compiler_params=pltpu.CompilerParams(
            collective_id=0, has_side_effects=True, vmem_limit_bytes=40 << 20
        ),
        cost_estimate=pl.CostEstimate(flops=1_200_000_000, bytes_accessed=6_000_000, transcendentals=0),
    )(upper_vals, upper_cols, result_cols)


def solution(mesh):
    in_specs = (
        P(("row", "col"), None, None, None),
        P(("row", "col"), None),
        P(("row", "col"), None),
    )
    out_specs = P(("row", "col"), None, None, None)
    return jax.shard_map(
        on_device, mesh=mesh, in_specs=in_specs, out_specs=out_specs, check_vma=False
    )
```

```python
import functools

import jax
import jax.numpy as jnp
from jax import lax
from jax.experimental import pallas as pl
from jax.experimental.pallas import tpu as pltpu
from jax.sharding import PartitionSpec as P

BLK = 128
REACH = 7
SLOTS = 6
NONE = SLOTS
ROWS = 2
STEPS = 2 * REACH
FIRST = REACH - 1
LAST = 2 * REACH
BEHIND = (-3, -2, -1)
AHEAD = (1, 2, 3, 4)
OTHERS = BEHIND + AHEAD
NEEDED = (
    {1: 5, 2: 4, 3: 2, -1: 6, -2: 6, -3: 6, -4: 6},
    {1: 5, 2: 5, 3: 3, -1: 6, -2: 6, -3: 6},
)
LANES = 4
TREES = {
    (0, 0): {-4: 0, -3: -4, -2: 2, -1: -4, 1: 0, 2: 1, 3: 0},
    (0, 1): {-3: 1, -2: -1, -1: 3, 1: 0, 2: 3, 3: 0},
    (1, 0): {-4: 0, -3: -4, -2: 2, -1: 0, 1: 0, 2: -1, 3: -1},
    (1, 1): {-3: 1, -2: -3, -1: 0, 1: 0, 2: -1, 3: -1},
    (2, 0): {-4: 0, -3: -4, -2: -1, -1: 0, 1: 0, 2: -2, 3: -1},
    (2, 1): {-3: 1, -2: 1, -1: 0, 1: 0, 2: 3, 3: -1},
    (3, 0): {-4: 0, -3: 0, -2: -3, -1: 0, 1: -3, 2: -2, 3: -1},
    (3, 1): {-3: 0, -2: -1, -1: 0, 1: -3, 2: 3, 3: -1},
}
ARRIVALS = {
    0: ((4, 0), (1, 0), (3, 0), (-3, 0), (1, 1), (3, 1), (-1, 0), (-3, 1), (2, 1), (2, 0), (-1, 1), (-2, 1), (-2, 0)),
    1: ((-1, 0), (4, 0), (1, 1), (-1, 1), (1, 0), (-3, 1), (2, 0), (2, 1), (3, 1), (-3, 0), (3, 0), (-2, 1), (-2, 0)),
    2: ((-1, 1), (4, 0), (1, 1), (-1, 0), (1, 0), (3, 1), (-2, 0), (-2, 1), (-3, 1), (-3, 0), (3, 0), (2, 1), (2, 0)),
    3: ((-3, 1), (-1, 1), (4, 0), (-3, 0), (-1, 0), (1, 1), (-2, 0), (3, 0), (3, 1), (1, 0), (2, 1), (-2, 1), (2, 0)),
}
FIRST_SENDS = {
    0: ((1, 0), (3, 1), (-4, 0), (1, 1), (3, 0)),
    1: ((-1, 0), (1, 1), (-4, 0), (-1, 1), (1, 0)),
    2: ((-1, 1), (-1, 0), (-4, 0), (1, 1), (1, 0)),
    3: ((-3, 0), (-1, 1), (-3, 1), (-1, 0), (-4, 0)),
}


def size(tree, needed, node):
    below = [size(tree, needed, n) for n, parent in tree.items() if parent == node]
    return max(below + [needed.get(node, 0)])


def hops(lane, distance, r):
    tree = TREES[(lane + distance) % LANES, r]
    return [
        (node + distance, -node, size(tree, NEEDED[r], node))
        for node, parent in tree.items()
        if parent == -distance
    ]


def band_kernel(device_total, block_total, vals, cols, kept, out, *scratch):
    held = dict(zip(OTHERS, scratch[:7]))
    places = dict(zip(OTHERS, scratch[7:14]))
    own, own_places, left, right, every, send_sem, recv_sem, psend_sem, precv_sem = scratch[14:]
    inner = lax.axis_size("col")
    me = lax.axis_index("row") * inner + lax.axis_index("col")

    def device(distance):
        there = lax.rem(me + distance + device_total, device_total)
        return (there // inner, lax.rem(there, inner))

    barrier = pltpu.get_barrier_semaphore()
    for m in (-4, -3, -2, -1, 1, 2, 3, 4):
        pl.semaphore_signal(barrier, inc=1, device_id=device(m), device_id_type=pl.DeviceIdType.MESH)

    zero = jnp.zeros((BLK, BLK), jnp.bfloat16)
    for r in range(ROWS):
        offs = [lax.rem(cols[r, s] - (me * ROWS + r) + block_total, block_total) for s in range(SLOTS)]
        ranks = [
            sum((offs[t] > offs[s]).astype(jnp.int32) for t in range(1, SLOTS) if t != s)
            for s in range(1, SLOTS)
        ]
        for j in range(SLOTS - 1):
            slot = sum(s * (ranks[s - 1] == j).astype(jnp.int32) for s in range(1, SLOTS))
            own[r, j] = vals[r, jnp.minimum(slot, SLOTS - 1)]
        own[r, SLOTS - 1] = vals[r, 0]
        own[r, NONE] = zero
        own_places[r, 0] = SLOTS - 1
        for o in range(1, REACH + 1):
            place = NONE
            for s in range(1, SLOTS):
                place = jnp.where(offs[s] == o, ranks[s - 1], place)
            own_places[r, o] = place
    for m in OTHERS:
        for r in range(ROWS):
            held[m][r, NONE] = zero

    pl.semaphore_wait(barrier, 8)

    def remote(source, target, r, count, send, distance, there):
        return pltpu.make_async_remote_copy(
            src_ref=source.at[r, pl.ds(0, count)],
            dst_ref=target.at[r, pl.ds(0, count)],
            send_sem=send_sem.at[send],
            recv_sem=recv_sem.at[OTHERS.index(there), r],
            device_id=device(distance),
            device_id_type=pl.DeviceIdType.MESH,
        )

    notes = []
    for k, m in enumerate(OTHERS):
        note = pltpu.make_async_remote_copy(
            src_ref=own_places,
            dst_ref=places[m],
            send_sem=psend_sem.at[k],
            recv_sem=precv_sem.at[k],
            device_id=device(-m),
            device_id_type=pl.DeviceIdType.MESH,
        )
        note.start()
        notes.append(note)

    def traffic(lane):
        sent = []

        def pass_on(m, r, only=None):
            source = own if m == 0 else held[m]
            for distance, there, count in hops(lane, m, r):
                if only in (None, distance):
                    copy = remote(source, held[there], r, count, len(sent), distance, there)
                    copy.start()
                    sent.append(copy)

        for distance, r in FIRST_SENDS[lane]:
            pass_on(0, r, distance)
        for m, r in ARRIVALS[lane]:
            count = size(TREES[(lane + m) % LANES, r], NEEDED[r], -m)
            remote(own, held[m], r, count, 0, 1, m).wait_recv()
            pass_on(m, r)
        for copy in sent:
            copy.wait_send()

    lane_here = lax.rem(me, LANES)
    for lane in range(LANES):
        pl.when(lane_here == lane)(functools.partial(traffic, lane))
    for note in notes:
        note.wait()

    def stored(row, offset):
        m, r = row // 2 - 3, row % 2
        if m == 0:
            return own[r, own_places[r, offset]]
        return held[m][r, places[m][r, offset]]

    def block(a, b):
        if a == b:
            d = stored(a, 0)
            return (d.astype(jnp.float32) + d.T.astype(jnp.float32)).astype(jnp.bfloat16)
        if abs(a - b) > REACH or min(a, b) > LAST:
            return zero
        if a < b:
            return stored(a, b - a)
        return stored(b, a - b).T

    for a in range(ROWS):
        for k in range(LAST + 2):
            lost = k > LAST or k < a
            left[pl.ds(a * BLK, BLK), pl.ds(k * BLK, BLK)] = zero if lost else block(FIRST + a, k)
    for p in range(REACH + 1):
        for k in range(2 * p, LAST + 2):
            for c in range(2):
                j = FIRST + 1 + 2 * p + c
                right[p, pl.ds(k * BLK, BLK), pl.ds(c * BLK, BLK)] = zero if k > LAST else block(k, j)
    for p in range(REACH + 1):
        deep = pl.ds(2 * p * BLK, (LAST + 2 - 2 * p) * BLK)
        got = jnp.dot(left[:, deep], right[p, deep, :], preferred_element_type=jnp.float32).astype(jnp.bfloat16)
        for a in range(ROWS):
            for c in range(2):
                step = 2 * p + c + 1 - a
                if 1 <= step <= STEPS:
                    every[a, step - 1] = got[a * BLK : (a + 1) * BLK, c * BLK : (c + 1) * BLK]
    for a in range(ROWS):
        for t in range(kept.shape[1]):
            step = lax.rem(kept[a, t] - (me * ROWS + a) + block_total, block_total)
            out[a, t] = every[a, jnp.clip(step - 1, 0, STEPS - 1)]


def on_device(upper_vals, upper_cols, result_cols):
    device_total = lax.axis_size("row") * lax.axis_size("col")
    rows, kept_count = result_cols.shape
    places_shape = pltpu.SMEM((ROWS, REACH + 1), jnp.int32)
    most_sent = max(
        sum(len(hops(lane, m, r)) for m, r in ARRIVALS[lane] + ((0, 0), (0, 1))) for lane in range(LANES)
    )

    def kernel(*refs):
        band_kernel(device_total, device_total * ROWS, *refs)

    return pl.pallas_call(
        kernel,
        out_shape=jax.ShapeDtypeStruct((rows, kept_count, BLK, BLK), jnp.bfloat16),
        in_specs=[
            pl.BlockSpec(memory_space=pltpu.VMEM),
            pl.BlockSpec(memory_space=pltpu.SMEM),
            pl.BlockSpec(memory_space=pltpu.SMEM),
        ],
        out_specs=pl.BlockSpec(memory_space=pltpu.VMEM),
        scratch_shapes=[
            *[pltpu.VMEM((ROWS, SLOTS + 1, BLK, BLK), jnp.bfloat16) for _ in OTHERS],
            *[places_shape for _ in OTHERS],
            pltpu.VMEM((ROWS, SLOTS + 1, BLK, BLK), jnp.bfloat16),
            places_shape,
            pltpu.VMEM((ROWS * BLK, (LAST + 2) * BLK), jnp.bfloat16),
            pltpu.VMEM((REACH + 1, (LAST + 2) * BLK, 2 * BLK), jnp.bfloat16),
            pltpu.VMEM((ROWS, STEPS, BLK, BLK), jnp.bfloat16),
            pltpu.SemaphoreType.DMA((most_sent,)),
            pltpu.SemaphoreType.DMA((len(OTHERS), ROWS)),
            pltpu.SemaphoreType.DMA((len(OTHERS),)),
            pltpu.SemaphoreType.DMA((len(OTHERS),)),
        ],
        compiler_params=pltpu.CompilerParams(
            collective_id=0, has_side_effects=True, vmem_limit_bytes=40 << 20
        ),
        cost_estimate=pl.CostEstimate(flops=1_200_000_000, bytes_accessed=6_000_000, transcendentals=0),
    )(upper_vals, upper_cols, result_cols)


def solution(mesh):
    in_specs = (
        P(("row", "col"), None, None, None),
        P(("row", "col"), None),
        P(("row", "col"), None),
    )
    out_specs = P(("row", "col"), None, None, None)
    return jax.shard_map(
        on_device, mesh=mesh, in_specs=in_specs, out_specs=out_specs, check_vma=False
    )
```

```python
import functools

import jax
import jax.numpy as jnp
from jax import lax
from jax.experimental import pallas as pl
from jax.experimental.pallas import tpu as pltpu
from jax.sharding import PartitionSpec as P

BLK = 128
REACH = 7
SLOTS = 6
NONE = SLOTS
ROWS = 2
STEPS = 2 * REACH
FIRST = REACH - 1
LAST = 2 * REACH
BEHIND = (-3, -2, -1)
AHEAD = (1, 2, 3, 4)
OTHERS = BEHIND + AHEAD
NEEDED = (
    {1: 5, 2: 4, 3: 2, -1: 6, -2: 6, -3: 6, -4: 6},
    {1: 5, 2: 5, 3: 3, -1: 6, -2: 6, -3: 6},
)
LANES = 4
TREES = {
    (0, 0): {-4: 0, -3: -4, -2: 2, -1: -4, 1: 0, 2: 1, 3: 0},
    (0, 1): {-3: 1, -2: -1, -1: 3, 1: 0, 2: 3, 3: 0},
    (1, 0): {-4: 0, -3: -4, -2: 2, -1: 0, 1: 0, 2: -1, 3: -1},
    (1, 1): {-3: 1, -2: -3, -1: 0, 1: 0, 2: -1, 3: -1},
    (2, 0): {-4: 0, -3: -4, -2: -1, -1: 0, 1: 0, 2: -2, 3: -1},
    (2, 1): {-3: 1, -2: 1, -1: 0, 1: 0, 2: 3, 3: -1},
    (3, 0): {-4: 0, -3: 0, -2: -3, -1: 0, 1: -3, 2: -2, 3: -1},
    (3, 1): {-3: 0, -2: -1, -1: 0, 1: -3, 2: 3, 3: -1},
}
ARRIVALS = {
    0: ((4, 0), (1, 0), (3, 0), (-3, 0), (1, 1), (3, 1), (-1, 0), (-3, 1), (2, 1), (2, 0), (-1, 1), (-2, 1), (-2, 0)),
    1: ((-1, 0), (4, 0), (1, 1), (-1, 1), (1, 0), (-3, 1), (2, 0), (2, 1), (3, 1), (-3, 0), (3, 0), (-2, 1), (-2, 0)),
    2: ((-1, 1), (4, 0), (1, 1), (-1, 0), (1, 0), (3, 1), (-2, 0), (-2, 1), (-3, 1), (-3, 0), (3, 0), (2, 1), (2, 0)),
    3: ((-3, 1), (-1, 1), (4, 0), (-3, 0), (-1, 0), (1, 1), (-2, 0), (3, 0), (3, 1), (1, 0), (2, 1), (-2, 1), (2, 0)),
}
FIRST_SENDS = {
    0: ((1, 0), (3, 1), (-4, 0), (1, 1), (3, 0)),
    1: ((-1, 0), (1, 1), (-4, 0), (-1, 1), (1, 0)),
    2: ((-1, 1), (-1, 0), (-4, 0), (1, 1), (1, 0)),
    3: ((-3, 0), (-1, 1), (-3, 1), (-1, 0), (-4, 0)),
}


def size(tree, needed, node):
    below = [size(tree, needed, n) for n, parent in tree.items() if parent == node]
    return max(below + [needed.get(node, 0)])


def hops(lane, distance, r):
    tree = TREES[(lane + distance) % LANES, r]
    return [
        (node + distance, -node, size(tree, NEEDED[r], node))
        for node, parent in tree.items()
        if parent == -distance
    ]


def band_kernel(device_total, block_total, vals_hbm, cols_hbm, kept_hbm, out, *scratch):
    held = dict(zip(OTHERS, scratch[:7]))
    places = dict(zip(OTHERS, scratch[7:14]))
    own, own_places, left, right, every, vals, cols, kept = scratch[14:22]
    send_sem, recv_sem, psend_sem, precv_sem, fetch_sem = scratch[22:]
    inner = lax.axis_size("col")
    me = lax.axis_index("row") * inner + lax.axis_index("col")

    def device(distance):
        there = lax.rem(me + distance + device_total, device_total)
        return (there // inner, lax.rem(there, inner))

    barrier = pltpu.get_barrier_semaphore()
    for m in (-4, -3, -2, -1, 1, 2, 3, 4):
        pl.semaphore_signal(barrier, inc=1, device_id=device(m), device_id_type=pl.DeviceIdType.MESH)

    fetches = [
        pltpu.make_async_copy(source, target, fetch_sem.at[k])
        for k, (source, target) in enumerate(((cols_hbm, cols), (vals_hbm, vals), (kept_hbm, kept)))
    ]
    for fetch in fetches:
        fetch.start()

    zero = jnp.zeros((BLK, BLK), jnp.bfloat16)
    for m in OTHERS:
        for r in range(ROWS):
            held[m][r, NONE] = zero
    fetches[0].wait()
    fetches[1].wait()
    for r in range(ROWS):
        offs = [lax.rem(cols[r, s] - (me * ROWS + r) + block_total, block_total) for s in range(SLOTS)]
        ranks = [
            sum((offs[t] > offs[s]).astype(jnp.int32) for t in range(1, SLOTS) if t != s)
            for s in range(1, SLOTS)
        ]
        for j in range(SLOTS - 1):
            slot = sum(s * (ranks[s - 1] == j).astype(jnp.int32) for s in range(1, SLOTS))
            own[r, j] = vals[r, jnp.minimum(slot, SLOTS - 1)]
        own[r, SLOTS - 1] = vals[r, 0]
        own[r, NONE] = zero
        own_places[r, 0] = SLOTS - 1
        for o in range(1, REACH + 1):
            place = NONE
            for s in range(1, SLOTS):
                place = jnp.where(offs[s] == o, ranks[s - 1], place)
            own_places[r, o] = place

    pl.semaphore_wait(barrier, 8)

    def remote(source, target, r, count, send, distance, there):
        return pltpu.make_async_remote_copy(
            src_ref=source.at[r, pl.ds(0, count)],
            dst_ref=target.at[r, pl.ds(0, count)],
            send_sem=send_sem.at[send],
            recv_sem=recv_sem.at[OTHERS.index(there), r],
            device_id=device(distance),
            device_id_type=pl.DeviceIdType.MESH,
        )

    def traffic(lane):
        sent = []

        def pass_on(m, r, only=None):
            source = own if m == 0 else held[m]
            for distance, there, count in hops(lane, m, r):
                if only in (None, distance):
                    copy = remote(source, held[there], r, count, len(sent), distance, there)
                    copy.start()
                    sent.append(copy)

        for distance, r in FIRST_SENDS[lane]:
            pass_on(0, r, distance)
        notes = []
        for k, m in enumerate(OTHERS):
            note = pltpu.make_async_remote_copy(
                src_ref=own_places,
                dst_ref=places[m],
                send_sem=psend_sem.at[k],
                recv_sem=precv_sem.at[k],
                device_id=device(-m),
                device_id_type=pl.DeviceIdType.MESH,
            )
            note.start()
            notes.append(note)
        for m, r in ARRIVALS[lane]:
            count = size(TREES[(lane + m) % LANES, r], NEEDED[r], -m)
            remote(own, held[m], r, count, 0, 1, m).wait_recv()
            pass_on(m, r)
        for copy in sent:
            copy.wait_send()
        for note in notes:
            note.wait()

    lane_here = lax.rem(me, LANES)
    for lane in range(LANES):
        pl.when(lane_here == lane)(functools.partial(traffic, lane))
    fetches[2].wait()

    def stored(row, offset):
        m, r = row // 2 - 3, row % 2
        if m == 0:
            return own[r, own_places[r, offset]]
        return held[m][r, places[m][r, offset]]

    def block(a, b):
        if a == b:
            d = stored(a, 0)
            return (d.astype(jnp.float32) + d.T.astype(jnp.float32)).astype(jnp.bfloat16)
        if abs(a - b) > REACH or min(a, b) > LAST:
            return zero
        if a < b:
            return stored(a, b - a)
        return stored(b, a - b).T

    for a in range(ROWS):
        for k in range(LAST + 2):
            lost = k > LAST or k < a
            left[pl.ds(a * BLK, BLK), pl.ds(k * BLK, BLK)] = zero if lost else block(FIRST + a, k)
    for p in range(REACH + 1):
        for k in range(2 * p, LAST + 2):
            for c in range(2):
                j = FIRST + 1 + 2 * p + c
                right[p, pl.ds(k * BLK, BLK), pl.ds(c * BLK, BLK)] = zero if k > LAST else block(k, j)
    for p in range(REACH + 1):
        deep = pl.ds(2 * p * BLK, (LAST + 2 - 2 * p) * BLK)
        got = jnp.dot(left[:, deep], right[p, deep, :], preferred_element_type=jnp.float32).astype(jnp.bfloat16)
        for a in range(ROWS):
            for c in range(2):
                step = 2 * p + c + 1 - a
                if 1 <= step <= STEPS:
                    every[a, step - 1] = got[a * BLK : (a + 1) * BLK, c * BLK : (c + 1) * BLK]
    for a in range(ROWS):
        for t in range(kept.shape[1]):
            step = lax.rem(kept[a, t] - (me * ROWS + a) + block_total, block_total)
            out[a, t] = every[a, jnp.clip(step - 1, 0, STEPS - 1)]


def on_device(upper_vals, upper_cols, result_cols):
    device_total = lax.axis_size("row") * lax.axis_size("col")
    rows, kept_count = result_cols.shape
    places_shape = pltpu.SMEM((ROWS, REACH + 1), jnp.int32)
    most_sent = max(
        sum(len(hops(lane, m, r)) for m, r in ARRIVALS[lane] + ((0, 0), (0, 1))) for lane in range(LANES)
    )

    def kernel(*refs):
        band_kernel(device_total, device_total * ROWS, *refs)

    return pl.pallas_call(
        kernel,
        out_shape=jax.ShapeDtypeStruct((rows, kept_count, BLK, BLK), jnp.bfloat16),
        in_specs=[
            pl.BlockSpec(memory_space=pltpu.HBM),
            pl.BlockSpec(memory_space=pltpu.HBM),
            pl.BlockSpec(memory_space=pltpu.HBM),
        ],
        out_specs=pl.BlockSpec(memory_space=pltpu.VMEM),
        scratch_shapes=[
            *[pltpu.VMEM((ROWS, SLOTS + 1, BLK, BLK), jnp.bfloat16) for _ in OTHERS],
            *[places_shape for _ in OTHERS],
            pltpu.VMEM((ROWS, SLOTS + 1, BLK, BLK), jnp.bfloat16),
            places_shape,
            pltpu.VMEM((ROWS * BLK, (LAST + 2) * BLK), jnp.bfloat16),
            pltpu.VMEM((REACH + 1, (LAST + 2) * BLK, 2 * BLK), jnp.bfloat16),
            pltpu.VMEM((ROWS, STEPS, BLK, BLK), jnp.bfloat16),
            pltpu.VMEM(upper_vals.shape, upper_vals.dtype),
            pltpu.SMEM(upper_cols.shape, upper_cols.dtype),
            pltpu.SMEM(result_cols.shape, result_cols.dtype),
            pltpu.SemaphoreType.DMA((most_sent,)),
            pltpu.SemaphoreType.DMA((len(OTHERS), ROWS)),
            pltpu.SemaphoreType.DMA((len(OTHERS),)),
            pltpu.SemaphoreType.DMA((len(OTHERS),)),
            pltpu.SemaphoreType.DMA((3,)),
        ],
        compiler_params=pltpu.CompilerParams(
            collective_id=0, has_side_effects=True, vmem_limit_bytes=40 << 20
        ),
        cost_estimate=pl.CostEstimate(flops=1_200_000_000, bytes_accessed=6_000_000, transcendentals=0),
    )(*(pltpu.with_memory_space_constraint(x, pltpu.HBM) for x in (upper_vals, upper_cols, result_cols)))


def solution(mesh):
    in_specs = (
        P(("row", "col"), None, None, None),
        P(("row", "col"), None),
        P(("row", "col"), None),
    )
    out_specs = P(("row", "col"), None, None, None)
    return jax.shard_map(
        on_device, mesh=mesh, in_specs=in_specs, out_specs=out_specs, check_vma=False
    )
```

```python
import functools

import jax
import jax.numpy as jnp
from jax import lax
from jax.experimental import pallas as pl
from jax.experimental.pallas import tpu as pltpu
from jax.sharding import PartitionSpec as P

BLK = 128
REACH = 7
SLOTS = 6
NONE = SLOTS
ROWS = 2
STEPS = 2 * REACH
FIRST = REACH - 1
LAST = 2 * REACH
PAIRS = REACH + 1
BEHIND = (-3, -2, -1)
AHEAD = (1, 2, 3, 4)
OTHERS = BEHIND + AHEAD
NEEDED = (
    {1: 5, 2: 4, 3: 2, -1: 6, -2: 6, -3: 6, -4: 6},
    {1: 5, 2: 5, 3: 3, -1: 6, -2: 6, -3: 6},
)
LANES = 4
TREES = {
    (0, 0): {-4: 0, -3: -4, -2: 2, -1: -4, 1: 0, 2: 1, 3: 0},
    (0, 1): {-3: 1, -2: -1, -1: 3, 1: 0, 2: 3, 3: 0},
    (1, 0): {-4: 0, -3: -4, -2: 2, -1: 0, 1: 0, 2: -1, 3: -1},
    (1, 1): {-3: 1, -2: -3, -1: 0, 1: 0, 2: -1, 3: -1},
    (2, 0): {-4: 0, -3: -4, -2: -1, -1: 0, 1: 0, 2: -2, 3: -1},
    (2, 1): {-3: 1, -2: 1, -1: 0, 1: 0, 2: 3, 3: -1},
    (3, 0): {-4: 0, -3: 0, -2: -3, -1: 0, 1: -3, 2: -2, 3: -1},
    (3, 1): {-3: 0, -2: -1, -1: 0, 1: -3, 2: 3, 3: -1},
}
ARRIVALS = {
    0: ((4, 0), (1, 0), (3, 0), (-3, 0), (1, 1), (3, 1), (-1, 0), (-3, 1), (2, 1), (2, 0), (-1, 1), (-2, 1), (-2, 0)),
    1: ((-1, 0), (4, 0), (1, 1), (-1, 1), (1, 0), (-3, 1), (2, 0), (2, 1), (3, 1), (-3, 0), (3, 0), (-2, 1), (-2, 0)),
    2: ((-1, 1), (4, 0), (1, 1), (-1, 0), (1, 0), (3, 1), (-2, 0), (-2, 1), (-3, 1), (-3, 0), (3, 0), (2, 1), (2, 0)),
    3: ((-3, 1), (-1, 1), (4, 0), (-3, 0), (-1, 0), (1, 1), (-2, 0), (3, 0), (3, 1), (1, 0), (2, 1), (-2, 1), (2, 0)),
}
FIRST_SENDS = {
    0: ((1, 0), (3, 1), (-4, 0), (1, 1), (3, 0)),
    1: ((-1, 0), (1, 1), (-4, 0), (-1, 1), (1, 0)),
    2: ((-1, 1), (-1, 0), (-4, 0), (1, 1), (1, 0)),
    3: ((-3, 0), (-1, 1), (-3, 1), (-1, 0), (-4, 0)),
}


def size(tree, needed, node):
    below = [size(tree, needed, n) for n, parent in tree.items() if parent == node]
    return max(below + [needed.get(node, 0)])


def hops(lane, distance, r):
    tree = TREES[(lane + distance) % LANES, r]
    return [
        (node + distance, -node, size(tree, NEEDED[r], node))
        for node, parent in tree.items()
        if parent == -distance
    ]


def band_kernel(device_total, block_total, vals_hbm, cols_hbm, kept_hbm, out, *scratch):
    held = {(m, r): scratch[i * ROWS + r] for i, m in enumerate((0, *OTHERS)) for r in range(ROWS)}
    places = dict(zip((0, *OTHERS), scratch[16:24]))
    left, right, sums, every, vals, cols, kept = scratch[24:31]
    send_sem, recv_sem, psend_sem, precv_sem, fetch_sem = scratch[31:]
    inner = lax.axis_size("col")
    me = lax.axis_index("row") * inner + lax.axis_index("col")

    def device(distance):
        there = lax.rem(me + distance + device_total, device_total)
        return (there // inner, lax.rem(there, inner))

    barrier = pltpu.get_barrier_semaphore()
    for m in (-4, -3, -2, -1, 1, 2, 3, 4):
        pl.semaphore_signal(barrier, inc=1, device_id=device(m), device_id_type=pl.DeviceIdType.MESH)
    fetches = [
        pltpu.make_async_copy(source, target, fetch_sem.at[k])
        for k, (source, target) in enumerate(((cols_hbm, cols), (vals_hbm, vals), (kept_hbm, kept)))
    ]
    for fetch in fetches:
        fetch.start()

    zero = jnp.zeros((BLK, BLK), jnp.bfloat16)
    for m in (0, *OTHERS):
        for r in range(ROWS):
            held[m, r][NONE] = zero
    fetches[0].wait()
    slots = []
    for r in range(ROWS):
        offs = [lax.rem(cols[r, s] - (me * ROWS + r) + block_total, block_total) for s in range(SLOTS)]
        ranks = [
            sum((offs[t] > offs[s]).astype(jnp.int32) for t in range(1, SLOTS) if t != s)
            for s in range(1, SLOTS)
        ]
        slots.append(
            [
                jnp.minimum(
                    sum(s * (ranks[s - 1] == j).astype(jnp.int32) for s in range(1, SLOTS)), SLOTS - 1
                )
                for j in range(SLOTS - 1)
            ]
        )
        places[0][r, 0] = SLOTS - 1
        for o in range(1, REACH + 1):
            place = NONE
            for s in range(1, SLOTS):
                place = jnp.where(offs[s] == o, ranks[s - 1], place)
            places[0][r, o] = place
    fetches[1].wait()
    for r in range(ROWS):
        for j in range(SLOTS - 1):
            held[0, r][j] = vals[r, slots[r][j]]
        held[0, r][SLOTS - 1] = vals[r, 0]
    fetches[2].wait()

    pl.semaphore_wait(barrier, 8)

    def remote(source, target, r, count, send, distance, there):
        return pltpu.make_async_remote_copy(
            src_ref=source.at[pl.ds(0, count)],
            dst_ref=target.at[pl.ds(0, count)],
            send_sem=send_sem.at[send],
            recv_sem=recv_sem.at[OTHERS.index(there), r],
            device_id=device(distance),
            device_id_type=pl.DeviceIdType.MESH,
        )

    def stored(row, offset):
        m, r = row // 2 - 3, row % 2
        return held[m, r][places[m][r, offset]]

    def block(a, b):
        if a == b:
            d = stored(a, 0)
            return (d.astype(jnp.float32) + d.T.astype(jnp.float32)).astype(jnp.bfloat16)
        if a < b:
            return stored(a, b - a)
        return stored(b, a - b).T

    def source(a, b):
        row = min(a, b)
        if abs(a - b) > REACH or row > LAST:
            return None
        return (row // 2 - 3, row % 2)

    def traffic(lane):
        sent = []
        here = {(0, 0), (0, 1), None}
        made = set()
        summed = {p: set() for p in range(PAIRS)}
        order = ARRIVALS[lane]
        last_relay = max(i for i, (m, r) in enumerate(order) if hops(lane, m, r))

        def pass_on(m, r, only=None):
            for distance, there, count in hops(lane, m, r):
                if only in (None, distance):
                    copy = remote(held[m, r], held[there, r], r, count, len(sent), distance, there)
                    copy.start()
                    sent.append(copy)

        def arrive(m, r):
            count = size(TREES[(lane + m) % LANES, r], NEEDED[r], -m)
            remote(held[0, r], held[m, r], r, count, 0, 1, m).wait_recv()
            here.add((m, r))

        def place(key, ref, at, a, b):
            if key not in made and source(a, b) in here:
                ref[at] = zero if source(a, b) is None else block(a, b)
                made.add(key)

        def assemble():
            for k in range(LAST + 2):
                for a in range(ROWS):
                    at = (pl.ds(a * BLK, BLK), pl.ds(k * BLK, BLK))
                    place(("left", a, k), left, at, FIRST + a, k)
                for p in range(k // 2 + 1):
                    for c in range(2):
                        at = (p, pl.ds(k * BLK, BLK), pl.ds(c * BLK, BLK))
                        place(("right", p, k, c), right, at, k, FIRST + 1 + 2 * p + c)

        def multiply():
            for p in range(PAIRS):
                ready = [
                    q
                    for q in range(p, PAIRS)
                    if q not in summed[p]
                    and all(("left", a, k) in made for a in range(ROWS) for k in (2 * q, 2 * q + 1))
                    and all(("right", p, k, c) in made for k in (2 * q, 2 * q + 1) for c in range(2))
                ]
                if not ready:
                    continue
                runs = []
                for q in ready:
                    if runs and runs[-1][1] == q:
                        runs[-1][1] = q + 1
                    else:
                        runs.append([q, q + 1])
                total = sums[p] if summed[p] else None
                for low, high in runs:
                    deep = pl.ds(2 * low * BLK, 2 * (high - low) * BLK)
                    part = jnp.dot(left[:, deep], right[p, deep, :], preferred_element_type=jnp.float32)
                    total = part if total is None else total + part
                summed[p].update(ready)
                if len(summed[p]) < PAIRS - p:
                    sums[p] = total
                    continue
                got = total.astype(jnp.bfloat16)
                for a in range(ROWS):
                    for c in range(2):
                        step = 2 * p + c + 1 - a
                        if 1 <= step <= STEPS:
                            every[a, step - 1] = got[a * BLK : (a + 1) * BLK, c * BLK : (c + 1) * BLK]

        for distance, r in FIRST_SENDS[lane]:
            pass_on(0, r, distance)
        notes = []
        for k, m in enumerate(OTHERS):
            note = pltpu.make_async_remote_copy(
                src_ref=places[0],
                dst_ref=places[m],
                send_sem=psend_sem.at[k],
                recv_sem=precv_sem.at[k],
                device_id=device(-m),
                device_id_type=pl.DeviceIdType.MESH,
            )
            note.start()
            notes.append(note)
        assemble()
        for m, r in order[: last_relay + 1]:
            arrive(m, r)
            pass_on(m, r)
        for note in notes:
            note.wait()
        for m, r in order[last_relay + 1 :]:
            assemble()
            multiply()
            arrive(m, r)
        assemble()
        multiply()
        for copy in sent:
            copy.wait_send()

    lane_here = lax.rem(me, LANES)
    for lane in range(LANES):
        pl.when(lane_here == lane)(functools.partial(traffic, lane))
    for a in range(ROWS):
        for t in range(kept.shape[1]):
            step = lax.rem(kept[a, t] - (me * ROWS + a) + block_total, block_total)
            out[a, t] = every[a, jnp.clip(step - 1, 0, STEPS - 1)]


def on_device(upper_vals, upper_cols, result_cols):
    device_total = lax.axis_size("row") * lax.axis_size("col")
    rows, kept_count = result_cols.shape
    places_shape = pltpu.SMEM((ROWS, REACH + 1), jnp.int32)
    most_sent = max(
        sum(len(hops(lane, m, r)) for m, r in ARRIVALS[lane] + ((0, 0), (0, 1))) for lane in range(LANES)
    )

    def kernel(*refs):
        band_kernel(device_total, device_total * ROWS, *refs)

    return pl.pallas_call(
        kernel,
        out_shape=jax.ShapeDtypeStruct((rows, kept_count, BLK, BLK), jnp.bfloat16),
        in_specs=[
            pl.BlockSpec(memory_space=pltpu.HBM),
            pl.BlockSpec(memory_space=pltpu.HBM),
            pl.BlockSpec(memory_space=pltpu.HBM),
        ],
        out_specs=pl.BlockSpec(memory_space=pltpu.VMEM),
        scratch_shapes=[
            *[pltpu.VMEM((SLOTS + 1, BLK, BLK), jnp.bfloat16) for _ in range(ROWS * (1 + len(OTHERS)))],
            *[places_shape for _ in range(1 + len(OTHERS))],
            pltpu.VMEM((ROWS * BLK, 2 * PAIRS * BLK), jnp.bfloat16),
            pltpu.VMEM((PAIRS, 2 * PAIRS * BLK, 2 * BLK), jnp.bfloat16),
            pltpu.VMEM((PAIRS, ROWS * BLK, 2 * BLK), jnp.float32),
            pltpu.VMEM((ROWS, STEPS, BLK, BLK), jnp.bfloat16),
            pltpu.VMEM(upper_vals.shape, upper_vals.dtype),
            pltpu.SMEM(upper_cols.shape, upper_cols.dtype),
            pltpu.SMEM(result_cols.shape, result_cols.dtype),
            pltpu.SemaphoreType.DMA((most_sent,)),
            pltpu.SemaphoreType.DMA((len(OTHERS), ROWS)),
            pltpu.SemaphoreType.DMA((len(OTHERS),)),
            pltpu.SemaphoreType.DMA((len(OTHERS),)),
            pltpu.SemaphoreType.DMA((3,)),
        ],
        compiler_params=pltpu.CompilerParams(
            collective_id=0, has_side_effects=True, vmem_limit_bytes=40 << 20
        ),
        cost_estimate=pl.CostEstimate(flops=1_200_000_000, bytes_accessed=6_000_000, transcendentals=0),
    )(*(pltpu.with_memory_space_constraint(x, pltpu.HBM) for x in (upper_vals, upper_cols, result_cols)))


def solution(mesh):
    in_specs = (
        P(("row", "col"), None, None, None),
        P(("row", "col"), None),
        P(("row", "col"), None),
    )
    out_specs = P(("row", "col"), None, None, None)
    return jax.shard_map(
        on_device, mesh=mesh, in_specs=in_specs, out_specs=out_specs, check_vma=False
    )
```

```python
import functools

import jax
import jax.numpy as jnp
from jax import lax
from jax.experimental import pallas as pl
from jax.experimental.pallas import tpu as pltpu
from jax.sharding import PartitionSpec as P

BLK = 128
REACH = 7
SLOTS = 6
NONE = SLOTS
ROWS = 2
STEPS = 2 * REACH
FIRST = REACH - 1
LAST = 2 * REACH
PAIRS = REACH + 1
BEHIND = (-3, -2, -1)
AHEAD = (1, 2, 3, 4)
OTHERS = BEHIND + AHEAD
NEEDED = (
    {1: 5, 2: 4, 3: 2, -1: 6, -2: 6, -3: 6, -4: 6},
    {1: 5, 2: 5, 3: 3, -1: 6, -2: 6, -3: 6},
)
TREES = {
    (0, 0): {3: 0, -3: -4, 2: 1, -2: -1, 1: 0, -1: -4, -4: 0},
    (0, 1): {3: 0, 2: 3, -3: 1, 1: 0, -1: 3, -2: -3},
    (1, 0): {-4: 0, 2: -1, 1: 0, -2: -3, 3: -1, -3: -4, -1: 0},
    (1, 1): {-2: 2, 3: -1, 2: 1, -3: 1, 1: 0, -1: 0},
    (2, 0): {2: -2, -3: -4, 3: -1, -4: 0, 1: -2, -2: -1, -1: 0},
    (2, 1): {1: 0, 3: -1, -3: 1, -2: 1, 2: 3, -1: 0},
    (3, 0): {3: -1, 1: -3, -4: 0, 2: -2, -3: 0, -1: 0, -2: -1},
    (3, 1): {3: -1, -2: -3, 1: -3, -3: 0, 2: 3, -1: 0},
}
ARRIVALS = {
    0: ((1, 1, 0), (4, 0, 0), (3, 1, 0), (1, 0, 0), (3, 0, 0), (4, 0, 1), (1, 1, 1), (3, 1, 1), (-3, 1, 0), (1, 0, 1), (3, 0, 1), (-1, 1, 0), (2, 0, 0), (-3, 0, 0), (2, 1, 0), (-1, 0, 0), (2, 0, 1), (2, 1, 1), (-1, 1, 1), (-2, 1, 0), (-1, 0, 1), (-2, 1, 1), (-2, 0, 0), (-2, 0, 1)),
    1: ((-1, 0, 0), (1, 0, 0), (4, 0, 0), (-1, 1, 0), (1, 1, 0), (4, 0, 1), (-1, 0, 1), (-3, 0, 0), (1, 0, 1), (-1, 1, 1), (1, 1, 1), (3, 1, 0), (-3, 1, 0), (2, 1, 0), (2, 0, 0), (3, 0, 0), (2, 0, 1), (-3, 1, 1), (3, 1, 1), (3, 0, 1), (-2, 1, 0), (-2, 0, 0), (2, 1, 1), (-2, 0, 1), (-2, 1, 1)),
    2: ((-1, 0, 0), (1, 0, 0), (4, 0, 0), (-1, 1, 0), (1, 1, 0), (4, 0, 1), (-1, 0, 1), (-3, 0, 0), (1, 0, 1), (-1, 1, 1), (1, 1, 1), (3, 1, 0), (-3, 1, 0), (-2, 0, 0), (-2, 1, 0), (3, 0, 0), (-2, 1, 1), (3, 1, 1), (-3, 1, 1), (3, 0, 1), (2, 0, 0), (-2, 0, 1), (2, 0, 1), (2, 1, 0), (2, 1, 1)),
    3: ((-3, 1, 0), (-1, 1, 0), (4, 0, 0), (-3, 0, 0), (-1, 1, 1), (4, 0, 1), (-3, 1, 1), (3, 0, 0), (1, 1, 0), (1, 0, 0), (3, 1, 0), (-2, 1, 0), (3, 0, 1), (-2, 0, 0), (3, 1, 1), (1, 0, 1), (-2, 0, 1), (-2, 1, 1), (1, 1, 1), (-1, 0, 0), (2, 0, 0), (2, 1, 0), (-1, 0, 1), (2, 1, 1), (2, 0, 1)),
}
FIRST_SENDS = {
    0: ((3, 1, 0), (3, 0, 0), (3, 1, 1), (1, 0, 0), (1, 1, 0), (1, 0, 1), (1, 1, 1), (-4, 0, 0), (-4, 0, 1)),
    1: ((-4, 0, 0), (-4, 0, 1), (1, 0, 0), (1, 1, 0), (1, 0, 1), (1, 1, 1), (-1, 1, 0), (-1, 0, 0), (-1, 1, 1), (-1, 0, 1)),
    2: ((-4, 0, 0), (-4, 0, 1), (1, 1, 0), (1, 1, 1), (-1, 0, 0), (-1, 1, 0), (-1, 0, 1), (-1, 1, 1)),
    3: ((-4, 0, 0), (-4, 0, 1), (-3, 1, 0), (-3, 0, 0), (-3, 1, 1), (-3, 0, 1), (-1, 0, 0), (-1, 1, 0), (-1, 0, 1), (-1, 1, 1)),
}
LANES = 4
FRONT = 3


def size(tree, needed, node):
    below = [size(tree, needed, n) for n, parent in tree.items() if parent == node]
    return max(below + [needed.get(node, 0)])


def parts(count):
    return [(0, count)] if count <= FRONT else [(0, FRONT), (FRONT, count - FRONT)]


def hops(lane, distance, r, part):
    tree = TREES[(lane + distance) % LANES, r]
    found = []
    for node, parent in tree.items():
        spans = parts(size(tree, NEEDED[r], node))
        if parent == -distance and part < len(spans):
            found.append((node + distance, -node, spans[part]))
    return found


def band_kernel(device_total, block_total, vals_hbm, cols_hbm, kept_hbm, out, *scratch):
    held = {(m, r): scratch[i * ROWS + r] for i, m in enumerate((0, *OTHERS)) for r in range(ROWS)}
    places = dict(zip((0, *OTHERS), scratch[16:24]))
    left, right, sums, every, vals, cols, kept = scratch[24:31]
    send_sem, recv_sem, psend_sem, precv_sem, fetch_sem = scratch[31:]
    inner = lax.axis_size("col")
    me = lax.axis_index("row") * inner + lax.axis_index("col")

    def device(distance):
        there = lax.rem(me + distance + device_total, device_total)
        return (there // inner, lax.rem(there, inner))

    barrier = pltpu.get_barrier_semaphore()
    for m in (-4, -3, -2, -1, 1, 2, 3, 4):
        pl.semaphore_signal(barrier, inc=1, device_id=device(m), device_id_type=pl.DeviceIdType.MESH)
    fetches = [
        pltpu.make_async_copy(source, target, fetch_sem.at[k])
        for k, (source, target) in enumerate(((cols_hbm, cols), (vals_hbm, vals), (kept_hbm, kept)))
    ]
    for fetch in fetches:
        fetch.start()

    zero = jnp.zeros((BLK, BLK), jnp.bfloat16)
    for m in (0, *OTHERS):
        for r in range(ROWS):
            held[m, r][NONE] = zero
    fetches[0].wait()
    slots = []
    for r in range(ROWS):
        offs = [lax.rem(cols[r, s] - (me * ROWS + r) + block_total, block_total) for s in range(SLOTS)]
        ranks = [
            sum((offs[t] > offs[s]).astype(jnp.int32) for t in range(1, SLOTS) if t != s)
            for s in range(1, SLOTS)
        ]
        slots.append(
            [
                jnp.minimum(
                    sum(s * (ranks[s - 1] == j).astype(jnp.int32) for s in range(1, SLOTS)), SLOTS - 1
                )
                for j in range(SLOTS - 1)
            ]
        )
        places[0][r, 0] = SLOTS - 1
        for o in range(1, REACH + 1):
            place = NONE
            for s in range(1, SLOTS):
                place = jnp.where(offs[s] == o, ranks[s - 1], place)
            places[0][r, o] = place
    fetches[1].wait()
    for r in range(ROWS):
        for j in range(SLOTS - 1):
            held[0, r][j] = vals[r, slots[r][j]]
        held[0, r][SLOTS - 1] = vals[r, 0]
    fetches[2].wait()

    pl.semaphore_wait(barrier, 8)

    def remote(source, target, r, span, send, distance, there):
        return pltpu.make_async_remote_copy(
            src_ref=source.at[pl.ds(*span)],
            dst_ref=target.at[pl.ds(*span)],
            send_sem=send_sem.at[send],
            recv_sem=recv_sem.at[OTHERS.index(there), r, 0 if span[0] == 0 else 1],
            device_id=device(distance),
            device_id_type=pl.DeviceIdType.MESH,
        )

    def stored(row, offset):
        m, r = row // 2 - 3, row % 2
        return held[m, r][places[m][r, offset]]

    def block(a, b):
        if a == b:
            d = stored(a, 0)
            return (d.astype(jnp.float32) + d.T.astype(jnp.float32)).astype(jnp.bfloat16)
        if a < b:
            return stored(a, b - a)
        return stored(b, a - b).T

    def source(a, b):
        row = min(a, b)
        if abs(a - b) > REACH or row > LAST:
            return None
        return (row // 2 - 3, row % 2)

    def traffic(lane):
        sent = []
        here = {(0, 0), (0, 1), None}
        made = set()
        summed = {p: set() for p in range(PAIRS)}
        order = ARRIVALS[lane]
        last_relay = max(i for i, item in enumerate(order) if hops(lane, *item))
        missing = {item: sum(item == (m, r) for m, r, _ in order) for item in {(m, r) for m, r, _ in order}}

        def pass_on(m, r, part, only=None):
            for distance, there, span in hops(lane, m, r, part):
                if only in (None, distance):
                    copy = remote(held[m, r], held[there, r], r, span, len(sent), distance, there)
                    copy.start()
                    sent.append(copy)

        def arrive(m, r, part):
            span = parts(size(TREES[(lane + m) % LANES, r], NEEDED[r], -m))[part]
            remote(held[0, r], held[m, r], r, span, 0, 1, m).wait_recv()
            missing[m, r] -= 1
            if not missing[m, r]:
                here.add((m, r))

        def place(key, ref, at, a, b):
            if key not in made and source(a, b) in here:
                ref[at] = zero if source(a, b) is None else block(a, b)
                made.add(key)

        def assemble():
            for k in range(LAST + 2):
                for a in range(ROWS):
                    at = (pl.ds(a * BLK, BLK), pl.ds(k * BLK, BLK))
                    place(("left", a, k), left, at, FIRST + a, k)
                for p in range(k // 2 + 1):
                    for c in range(2):
                        at = (p, pl.ds(k * BLK, BLK), pl.ds(c * BLK, BLK))
                        place(("right", p, k, c), right, at, k, FIRST + 1 + 2 * p + c)

        def multiply():
            for p in range(PAIRS):
                ready = [
                    q
                    for q in range(p, PAIRS)
                    if q not in summed[p]
                    and all(("left", a, k) in made for a in range(ROWS) for k in (2 * q, 2 * q + 1))
                    and all(("right", p, k, c) in made for k in (2 * q, 2 * q + 1) for c in range(2))
                ]
                if not ready:
                    continue
                runs = []
                for q in ready:
                    if runs and runs[-1][1] == q:
                        runs[-1][1] = q + 1
                    else:
                        runs.append([q, q + 1])
                total = sums[p] if summed[p] else None
                for low, high in runs:
                    deep = pl.ds(2 * low * BLK, 2 * (high - low) * BLK)
                    part = jnp.dot(left[:, deep], right[p, deep, :], preferred_element_type=jnp.float32)
                    total = part if total is None else total + part
                summed[p].update(ready)
                if len(summed[p]) < PAIRS - p:
                    sums[p] = total
                    continue
                got = total.astype(jnp.bfloat16)
                for a in range(ROWS):
                    for c in range(2):
                        step = 2 * p + c + 1 - a
                        if 1 <= step <= STEPS:
                            every[a, step - 1] = got[a * BLK : (a + 1) * BLK, c * BLK : (c + 1) * BLK]

        for distance, r, part in FIRST_SENDS[lane]:
            pass_on(0, r, part, distance)
        notes = []
        for k, m in enumerate(OTHERS):
            note = pltpu.make_async_remote_copy(
                src_ref=places[0],
                dst_ref=places[m],
                send_sem=psend_sem.at[k],
                recv_sem=precv_sem.at[k],
                device_id=device(-m),
                device_id_type=pl.DeviceIdType.MESH,
            )
            note.start()
            notes.append(note)
        assemble()
        for item in order[: last_relay + 1]:
            arrive(*item)
            pass_on(*item)
        for note in notes:
            note.wait()
        for item in order[last_relay + 1 :]:
            assemble()
            multiply()
            arrive(*item)
        assemble()
        multiply()
        for copy in sent:
            copy.wait_send()

    lane_here = lax.rem(me, LANES)
    for lane in range(LANES):
        pl.when(lane_here == lane)(functools.partial(traffic, lane))
    for a in range(ROWS):
        for t in range(kept.shape[1]):
            step = lax.rem(kept[a, t] - (me * ROWS + a) + block_total, block_total)
            out[a, t] = every[a, jnp.clip(step - 1, 0, STEPS - 1)]


def on_device(upper_vals, upper_cols, result_cols):
    device_total = lax.axis_size("row") * lax.axis_size("col")
    rows, kept_count = result_cols.shape
    places_shape = pltpu.SMEM((ROWS, REACH + 1), jnp.int32)
    most_sent = max(
        len(FIRST_SENDS[lane]) + sum(len(hops(lane, *item)) for item in ARRIVALS[lane]) for lane in range(LANES)
    )

    def kernel(*refs):
        band_kernel(device_total, device_total * ROWS, *refs)

    return pl.pallas_call(
        kernel,
        out_shape=jax.ShapeDtypeStruct((rows, kept_count, BLK, BLK), jnp.bfloat16),
        in_specs=[
            pl.BlockSpec(memory_space=pltpu.HBM),
            pl.BlockSpec(memory_space=pltpu.HBM),
            pl.BlockSpec(memory_space=pltpu.HBM),
        ],
        out_specs=pl.BlockSpec(memory_space=pltpu.VMEM),
        scratch_shapes=[
            *[pltpu.VMEM((SLOTS + 1, BLK, BLK), jnp.bfloat16) for _ in range(ROWS * (1 + len(OTHERS)))],
            *[places_shape for _ in range(1 + len(OTHERS))],
            pltpu.VMEM((ROWS * BLK, 2 * PAIRS * BLK), jnp.bfloat16),
            pltpu.VMEM((PAIRS, 2 * PAIRS * BLK, 2 * BLK), jnp.bfloat16),
            pltpu.VMEM((PAIRS, ROWS * BLK, 2 * BLK), jnp.float32),
            pltpu.VMEM((ROWS, STEPS, BLK, BLK), jnp.bfloat16),
            pltpu.VMEM(upper_vals.shape, upper_vals.dtype),
            pltpu.SMEM(upper_cols.shape, upper_cols.dtype),
            pltpu.SMEM(result_cols.shape, result_cols.dtype),
            pltpu.SemaphoreType.DMA((most_sent,)),
            pltpu.SemaphoreType.DMA((len(OTHERS), ROWS, 2)),
            pltpu.SemaphoreType.DMA((len(OTHERS),)),
            pltpu.SemaphoreType.DMA((len(OTHERS),)),
            pltpu.SemaphoreType.DMA((3,)),
        ],
        compiler_params=pltpu.CompilerParams(
            collective_id=0, has_side_effects=True, vmem_limit_bytes=40 << 20
        ),
        cost_estimate=pl.CostEstimate(flops=1_200_000_000, bytes_accessed=6_000_000, transcendentals=0),
    )(*(pltpu.with_memory_space_constraint(x, pltpu.HBM) for x in (upper_vals, upper_cols, result_cols)))


def solution(mesh):
    in_specs = (
        P(("row", "col"), None, None, None),
        P(("row", "col"), None),
        P(("row", "col"), None),
    )
    out_specs = P(("row", "col"), None, None, None)
    return jax.shard_map(
        on_device, mesh=mesh, in_specs=in_specs, out_specs=out_specs, check_vma=False
    )
```

```python
import functools

import jax
import jax.numpy as jnp
from jax import lax
from jax.experimental import pallas as pl
from jax.experimental.pallas import tpu as pltpu
from jax.sharding import PartitionSpec as P

BLK = 128
REACH = 7
SLOTS = 6
NONE = SLOTS
ROWS = 2
STEPS = 2 * REACH
FIRST = REACH - 1
LAST = 2 * REACH
PAIRS = REACH + 1
BEHIND = (-3, -2, -1)
AHEAD = (1, 2, 3, 4)
OTHERS = BEHIND + AHEAD
NEEDED = (
    {1: 5, 2: 4, 3: 2, -1: 6, -2: 6, -3: 6, -4: 6},
    {1: 5, 2: 5, 3: 3, -1: 6, -2: 6, -3: 6},
)
PARTS = ((0, 3), (3, 6))
HALF = BLK // 2
PACKED = HALF + 16
UNIT = 16
UNITS = BLK // UNIT
TREES = {
    (0, 0, 0): {3: 0, -1: -4, -2: -3, -3: -4, -4: 0, 2: 1, 1: 0},
    (0, 0, 1): {2: 0, -3: -4, -1: -4, -2: -3, -4: 0, 1: -3},
    (0, 1, 0): {3: 0, -3: 1, 2: 3, -1: 3, -2: 2, 1: 0},
    (0, 1, 1): {2: 1, 1: 0, -2: -3, -1: -3, -3: 1},
    (1, 0, 0): {-1: 0, 3: 2, -3: -4, 1: 2, 2: -1, -4: 0, -2: 2},
    (1, 0, 1): {-3: -4, -4: 0, 2: -1, 1: 2, -1: 0, -2: -3},
    (1, 1, 0): {-3: 1, -1: 0, -2: -3, 2: 1, 1: 0, 3: -1},
    (1, 1, 1): {1: 0, -2: -3, -1: 0, 2: 1, -3: 1},
    (2, 0, 0): {-2: -1, 2: -2, -4: 0, -3: -4, 1: -2, -1: 0, 3: -1},
    (2, 0, 1): {1: -3, 2: -1, -1: 0, -4: 0, -2: -1, -3: -4},
    (2, 1, 0): {1: 0, 2: 3, -2: 1, -3: 1, -1: 0, 3: -1},
    (2, 1, 1): {2: 1, -3: 1, -1: 0, 1: 0, -2: 1},
    (3, 0, 0): {-4: 0, 1: -3, 2: 1, -2: -1, -1: 0, -3: 0, 3: -1},
    (3, 0, 1): {-1: 0, 1: -3, -3: 0, 2: 1, -4: 0, -2: -1},
    (3, 1, 0): {-2: -3, 2: 3, -1: 0, 3: -1, -3: 0, 1: -3},
    (3, 1, 1): {-1: 0, -3: 0, -2: -3, 1: -3, 2: -1},
}
ARRIVALS = {
    0: ((1, 0, 0), (3, 0, 1), (4, 0, 0), (1, 1, 0), (4, 0, 1), (3, 0, 0), (-1, 0, 1), (1, 1, 1), (3, 1, 1), (1, 0, 1), (3, 1, 0), (-1, 0, 0), (-3, 1, 0), (2, 0, 0), (2, 1, 0), (-2, 1, 1), (-1, 1, 1), (2, 0, 1), (-2, 0, 1), (2, 1, 1), (-1, 1, 0), (-3, 0, 0), (-2, 0, 0), (-2, 1, 0)),
    1: ((-1, 1, 1), (4, 0, 1), (1, 0, 0), (-1, 0, 0), (4, 0, 0), (1, 1, 0), (-1, 1, 0), (1, 0, 1), (3, 1, 1), (-3, 0, 0), (3, 0, 0), (1, 1, 1), (-3, 1, 0), (2, 0, 1), (3, 0, 1), (3, 1, 0), (-2, 0, 1), (2, 1, 1), (-2, 1, 1), (-2, 1, 0), (-1, 0, 1), (2, 0, 0), (2, 1, 0), (-2, 0, 0)),
    2: ((-1, 1, 1), (1, 0, 1), (4, 0, 0), (-1, 1, 0), (1, 1, 0), (4, 0, 1), (-2, 1, 1), (1, 1, 1), (3, 1, 1), (-2, 0, 1), (3, 0, 1), (1, 0, 0), (-3, 1, 0), (3, 1, 0), (-2, 0, 0), (3, 0, 0), (-2, 1, 0), (-1, 0, 0), (-3, 0, 0), (2, 1, 1), (2, 0, 0), (2, 1, 0), (-1, 0, 1), (2, 0, 1)),
    3: ((-3, 0, 0), (-1, 1, 0), (4, 0, 0), (-3, 1, 0), (-1, 1, 1), (4, 0, 1), (-2, 1, 1), (3, 1, 0), (-2, 0, 0), (3, 0, 0), (1, 0, 0), (1, 1, 0), (1, 0, 1), (-2, 1, 0), (3, 0, 1), (3, 1, 1), (-2, 0, 1), (2, 1, 1), (2, 0, 0), (-1, 0, 0), (2, 0, 1), (1, 1, 1), (-1, 0, 1), (2, 1, 0)),
}
FIRST_SENDS = {
    0: ((3, 0, 0), (3, 1, 0), (2, 0, 1), (1, 1, 1), (-4, 0, 0), (1, 0, 0), (-4, 0, 1), (1, 1, 0)),
    1: ((-1, 0, 0), (-1, 1, 0), (1, 1, 1), (-1, 1, 1), (-4, 0, 1), (-4, 0, 0), (1, 1, 0), (-1, 0, 1)),
    2: ((1, 1, 0), (-4, 0, 0), (-1, 0, 0), (-1, 1, 0), (-1, 0, 1), (-4, 0, 1), (-1, 1, 1), (1, 1, 1)),
    3: ((-1, 0, 1), (-3, 0, 1), (-4, 0, 0), (-1, 1, 0), (-1, 1, 1), (-4, 0, 1), (-1, 0, 0), (-3, 0, 0), (-3, 1, 1), (-3, 1, 0)),
}
LANES = 4


def size(lane, r, part, node):
    first, end = PARTS[part]
    mine = max(min(NEEDED[r].get(node, 0), end) - first, 0)
    below = [size(lane, r, part, n) for n, parent in TREES[lane, r, part].items() if parent == node]
    return max(below + [mine])


def hops(lane, distance, r, part):
    tree = TREES[(lane + distance) % LANES, r, part]
    return [(node + distance, -node) for node, parent in tree.items() if parent == -distance]


def halves(shape):
    return (lax.broadcasted_iota(jnp.int32, shape, axis) for axis in (0, 1))


def packed(whole):
    whole = whole.astype(jnp.float32)
    upper, lower = whole[:HALF], pltpu.roll(whole[HALF:], HALF, axis=1)
    i, j = halves((HALF, BLK))
    middle = jnp.sum(jnp.where(i == j, lower, 0.0), axis=0, keepdims=True)
    return (
        jnp.where(i > j, lower, upper).astype(jnp.bfloat16),
        jnp.broadcast_to(middle, (PACKED - HALF, BLK)).astype(jnp.bfloat16),
    )


def unpacked(rows, middle):
    rows, middle = rows.astype(jnp.float32), middle.astype(jnp.float32)[:1]
    turned = jnp.concatenate([rows, jnp.zeros_like(rows)], axis=0).T
    i, j = halves((HALF, BLK))
    upper = jnp.where(i <= j, rows, turned[:HALF])
    lower = jnp.where(i > j, rows, jnp.where(i == j, middle, turned[:HALF]))
    lower = jnp.where(j < HALF, turned[HALF:], pltpu.roll(lower, HALF, axis=1))
    return jnp.concatenate([upper, lower], axis=0).astype(jnp.bfloat16)


def band_kernel(device_total, block_total, vals_hbm, cols_hbm, kept_hbm, out, *scratch):
    held = {(m, r): scratch[i * ROWS + r] for i, m in enumerate((0, *OTHERS)) for r in range(ROWS)}
    places = dict(zip((0, *OTHERS), scratch[16:24]))
    left, right, sums, every, vals, cols, kept, middles = scratch[24:32]
    send_sem, recv_sem, psend_sem, precv_sem, fetch_sem = scratch[32:]
    inner = lax.axis_size("col")
    me = lax.axis_index("row") * inner + lax.axis_index("col")

    def device(distance):
        there = lax.rem(me + distance + device_total, device_total)
        return (there // inner, lax.rem(there, inner))

    barrier = pltpu.get_barrier_semaphore()
    for m in (-4, -3, -2, -1, 1, 2, 3, 4):
        pl.semaphore_signal(barrier, inc=1, device_id=device(m), device_id_type=pl.DeviceIdType.MESH)
    fetches = [
        pltpu.make_async_copy(source, target, fetch_sem.at[k])
        for k, (source, target) in enumerate(((cols_hbm, cols), (vals_hbm, vals), (kept_hbm, kept)))
    ]
    for fetch in fetches:
        fetch.start()

    zero = jnp.zeros((BLK, BLK), jnp.bfloat16)
    for m in (0, *OTHERS):
        for r in range(ROWS):
            held[m, r][pl.ds(NONE * UNITS, UNITS)] = zero.reshape(UNITS, UNIT, BLK)
    fetches[0].wait()
    slots = []
    for r in range(ROWS):
        offs = [lax.rem(cols[r, s] - (me * ROWS + r) + block_total, block_total) for s in range(SLOTS)]
        ranks = [
            sum((offs[t] > offs[s]).astype(jnp.int32) for t in range(1, SLOTS) if t != s)
            for s in range(1, SLOTS)
        ]
        slots.append(
            [
                jnp.minimum(
                    sum(s * (ranks[s - 1] == j).astype(jnp.int32) for s in range(1, SLOTS)), SLOTS - 1
                )
                for j in range(SLOTS - 1)
            ]
        )
        places[0][r, 0] = 0
        for o in range(1, REACH + 1):
            place = NONE
            for s in range(1, SLOTS):
                place = jnp.where(offs[s] == o, ranks[s - 1], place)
            places[0][r, o] = place
    fetches[1].wait()
    for r in range(ROWS):
        for j in range(SLOTS - 1):
            held[0, r][pl.ds(j * UNITS, UNITS)] = vals[r, slots[r][j]].reshape(UNITS, UNIT, BLK)
        middle = vals[r, 0]
        middle = (middle.astype(jnp.float32) + middle.T.astype(jnp.float32)).astype(jnp.bfloat16)
        middles[r] = middle
        rows, last = packed(middle)
        held[0, r][pl.ds((SLOTS - 1) * UNITS, UNITS // 2)] = rows.reshape(UNITS // 2, UNIT, BLK)
        held[0, r][(SLOTS - 1) * UNITS + UNITS // 2] = last
    fetches[2].wait()

    pl.semaphore_wait(barrier, 8)

    def remote(lane, m, there, r, part, send, distance):
        blocks = size((lane + m) % LANES, r, part, -there)
        rows = blocks * BLK - (BLK - PACKED if PARTS[part][0] + blocks == SLOTS else 0)
        span = pl.ds(PARTS[part][0] * UNITS, rows // UNIT)
        return pltpu.make_async_remote_copy(
            src_ref=held[m, r].at[span],
            dst_ref=held[there, r].at[span],
            send_sem=send_sem.at[send],
            recv_sem=recv_sem.at[OTHERS.index(there), r, part],
            device_id=device(distance),
            device_id_type=pl.DeviceIdType.MESH,
        )

    def stored(row, offset):
        m, r = row // 2 - 3, row % 2
        first = places[m][r, offset] * UNITS
        return jnp.concatenate([held[m, r][first + k] for k in range(UNITS)], axis=0)

    def block(a, b):
        if a == b:
            m, r = a // 2 - 3, a % 2
            if m == 0:
                return middles[r]
            first = (SLOTS - 1) * UNITS
            rows = held[m, r][pl.ds(first, UNITS // 2)].reshape(HALF, BLK)
            return unpacked(rows, held[m, r][first + UNITS // 2])
        if a < b:
            return stored(a, b - a)
        return stored(b, a - b).T

    def source(a, b):
        row = min(a, b)
        if abs(a - b) > REACH or row > LAST:
            return None
        return (row // 2 - 3, row % 2)

    def traffic(lane):
        sent = []
        here = {(0, 0), (0, 1), None}
        made = set()
        summed = {p: set() for p in range(PAIRS)}
        order = ARRIVALS[lane]
        last_relay = max(i for i, item in enumerate(order) if hops(lane, *item))
        missing = {item: sum(item == (m, r) for m, r, _ in order) for item in {(m, r) for m, r, _ in order}}

        def pass_on(m, r, part, only=None):
            for distance, there in hops(lane, m, r, part):
                if only in (None, distance):
                    copy = remote(lane, m, there, r, part, len(sent), distance)
                    copy.start()
                    sent.append(copy)

        def arrive(m, r, part):
            remote(lane, m, m, r, part, 0, 1).wait_recv()
            missing[m, r] -= 1
            if not missing[m, r]:
                here.add((m, r))

        def place(key, ref, at, a, b):
            if key not in made and source(a, b) in here:
                ref[at] = zero if source(a, b) is None else block(a, b)
                made.add(key)

        def assemble():
            for k in range(LAST + 2):
                for a in range(ROWS):
                    at = (pl.ds(a * BLK, BLK), pl.ds(k * BLK, BLK))
                    place(("left", a, k), left, at, FIRST + a, k)
                for p in range(k // 2 + 1):
                    for c in range(2):
                        at = (p, pl.ds(k * BLK, BLK), pl.ds(c * BLK, BLK))
                        place(("right", p, k, c), right, at, k, FIRST + 1 + 2 * p + c)

        def multiply():
            for p in range(PAIRS):
                ready = [
                    q
                    for q in range(p, PAIRS)
                    if q not in summed[p]
                    and all(("left", a, k) in made for a in range(ROWS) for k in (2 * q, 2 * q + 1))
                    and all(("right", p, k, c) in made for k in (2 * q, 2 * q + 1) for c in range(2))
                ]
                if not ready:
                    continue
                runs = []
                for q in ready:
                    if runs and runs[-1][1] == q:
                        runs[-1][1] = q + 1
                    else:
                        runs.append([q, q + 1])
                total = sums[p] if summed[p] else None
                for low, high in runs:
                    deep = pl.ds(2 * low * BLK, 2 * (high - low) * BLK)
                    part = jnp.dot(left[:, deep], right[p, deep, :], preferred_element_type=jnp.float32)
                    total = part if total is None else total + part
                summed[p].update(ready)
                if len(summed[p]) < PAIRS - p:
                    sums[p] = total
                    continue
                got = total.astype(jnp.bfloat16)
                for a in range(ROWS):
                    for c in range(2):
                        step = 2 * p + c + 1 - a
                        if 1 <= step <= STEPS:
                            every[a, step - 1] = got[a * BLK : (a + 1) * BLK, c * BLK : (c + 1) * BLK]

        for distance, r, part in FIRST_SENDS[lane]:
            pass_on(0, r, part, distance)
        notes = []
        for k, m in enumerate(OTHERS):
            note = pltpu.make_async_remote_copy(
                src_ref=places[0],
                dst_ref=places[m],
                send_sem=psend_sem.at[k],
                recv_sem=precv_sem.at[k],
                device_id=device(-m),
                device_id_type=pl.DeviceIdType.MESH,
            )
            note.start()
            notes.append(note)
        assemble()
        for item in order[: last_relay + 1]:
            arrive(*item)
            pass_on(*item)
        for note in notes:
            note.wait()
        for item in order[last_relay + 1 :]:
            assemble()
            multiply()
            arrive(*item)
        assemble()
        multiply()
        for copy in sent:
            copy.wait_send()

    lane_here = lax.rem(me, LANES)
    for lane in range(LANES):
        pl.when(lane_here == lane)(functools.partial(traffic, lane))
    for a in range(ROWS):
        for t in range(kept.shape[1]):
            step = lax.rem(kept[a, t] - (me * ROWS + a) + block_total, block_total)
            out[a, t] = every[a, jnp.clip(step - 1, 0, STEPS - 1)]


def on_device(upper_vals, upper_cols, result_cols):
    device_total = lax.axis_size("row") * lax.axis_size("col")
    rows, kept_count = result_cols.shape
    places_shape = pltpu.SMEM((ROWS, REACH + 1), jnp.int32)
    most_sent = max(
        len(FIRST_SENDS[lane]) + sum(len(hops(lane, *item)) for item in ARRIVALS[lane]) for lane in range(LANES)
    )

    def kernel(*refs):
        band_kernel(device_total, device_total * ROWS, *refs)

    return pl.pallas_call(
        kernel,
        out_shape=jax.ShapeDtypeStruct((rows, kept_count, BLK, BLK), jnp.bfloat16),
        in_specs=[
            pl.BlockSpec(memory_space=pltpu.HBM),
            pl.BlockSpec(memory_space=pltpu.HBM),
            pl.BlockSpec(memory_space=pltpu.HBM),
        ],
        out_specs=pl.BlockSpec(memory_space=pltpu.VMEM),
        scratch_shapes=[
            *[pltpu.VMEM(((SLOTS + 1) * UNITS, UNIT, BLK), jnp.bfloat16) for _ in range(ROWS * (1 + len(OTHERS)))],
            *[places_shape for _ in range(1 + len(OTHERS))],
            pltpu.VMEM((ROWS * BLK, 2 * PAIRS * BLK), jnp.bfloat16),
            pltpu.VMEM((PAIRS, 2 * PAIRS * BLK, 2 * BLK), jnp.bfloat16),
            pltpu.VMEM((PAIRS, ROWS * BLK, 2 * BLK), jnp.float32),
            pltpu.VMEM((ROWS, STEPS, BLK, BLK), jnp.bfloat16),
            pltpu.VMEM(upper_vals.shape, upper_vals.dtype),
            pltpu.SMEM(upper_cols.shape, upper_cols.dtype),
            pltpu.SMEM(result_cols.shape, result_cols.dtype),
            pltpu.VMEM((ROWS, BLK, BLK), jnp.bfloat16),
            pltpu.SemaphoreType.DMA((most_sent,)),
            pltpu.SemaphoreType.DMA((len(OTHERS), ROWS, 2)),
            pltpu.SemaphoreType.DMA((len(OTHERS),)),
            pltpu.SemaphoreType.DMA((len(OTHERS),)),
            pltpu.SemaphoreType.DMA((3,)),
        ],
        compiler_params=pltpu.CompilerParams(
            collective_id=0, has_side_effects=True, vmem_limit_bytes=40 << 20
        ),
        cost_estimate=pl.CostEstimate(flops=1_200_000_000, bytes_accessed=6_000_000, transcendentals=0),
    )(*(pltpu.with_memory_space_constraint(x, pltpu.HBM) for x in (upper_vals, upper_cols, result_cols)))


def solution(mesh):
    in_specs = (
        P(("row", "col"), None, None, None),
        P(("row", "col"), None),
        P(("row", "col"), None),
    )
    out_specs = P(("row", "col"), None, None, None)
    return jax.shard_map(
        on_device, mesh=mesh, in_specs=in_specs, out_specs=out_specs, check_vma=False
    )
```

```python
import functools

import jax
import jax.numpy as jnp
from jax import lax
from jax.experimental import pallas as pl
from jax.experimental.pallas import tpu as pltpu
from jax.sharding import PartitionSpec as P

BLK = 128
REACH = 7
SLOTS = 6
NONE = SLOTS
ROWS = 2
STEPS = 2 * REACH
FIRST = REACH - 1
LAST = 2 * REACH
PAIRS = REACH + 1
BEHIND = (-3, -2, -1)
AHEAD = (1, 2, 3, 4)
OTHERS = BEHIND + AHEAD
NEEDED = (
    {1: 5, 2: 4, 3: 2, -1: 6, -2: 6, -3: 6, -4: 6},
    {1: 5, 2: 5, 3: 3, -1: 6, -2: 6, -3: 6},
)
PARTS = ((0, 3), (3, 6))
HALF = BLK // 2
PACKED = HALF + 16
UNIT = 16
UNITS = BLK // UNIT
TREES = {
    (0, 0, 0): {-1: -4, 3: -1, 1: 0, -4: 0, -3: -4, -2: -3, 2: 1},
    (0, 0, 1): {2: 3, -3: -4, 1: -3, -4: 0, -2: -3, 3: 0, -1: -4},
    (0, 1, 0): {3: 0, -1: 3, 2: 3, -2: 2, 1: 0, -3: 1},
    (0, 1, 1): {-3: 1, 1: 0, 3: 0, -1: 3, -2: -1, 2: 3},
    (1, 0, 0): {-1: 0, 1: 2, 2: -1, -2: -3, 3: -1, -4: 0, -3: -4},
    (1, 0, 1): {1: -3, -1: 0, 2: -1, -4: 0, -3: -4, -2: 2},
    (1, 1, 0): {1: 0, -2: -3, 3: -1, -3: 1, 2: -1, -1: 0},
    (1, 1, 1): {2: -1, -3: 0, 1: 0, -2: -3, -1: 0},
    (2, 0, 0): {-2: 1, 1: 0, 2: -2, -4: 0, 3: -1, -3: -4, -1: 0},
    (2, 0, 1): {1: 0, -1: 0, 2: -1, -2: -1, -3: -4, -4: 0},
    (2, 1, 0): {3: -1, 1: 0, -3: 1, 2: 3, -2: -1, -1: 0},
    (2, 1, 1): {-1: 0, 2: 1, -2: 1, 1: 0, -3: 1},
    (3, 0, 0): {-2: -1, 3: -1, -4: 0, 2: 1, -3: 0, 1: -3, -1: 0},
    (3, 0, 1): {2: 1, -2: -1, -3: 0, -1: 0, -4: 0, 1: -3},
    (3, 1, 0): {3: -1, 2: 3, -1: 0, -3: 0, 1: -3, -2: -3},
    (3, 1, 1): {3: -1, 1: -3, -3: 0, -1: 0, -2: -3, 2: 3},
}
ARRIVALS = {
    0: ((1, 0, 0), (3, 0, 1), (4, 0, 0), (1, 0, 1), (3, 0, 0), (4, 0, 1), (3, 1, 1), (1, 1, 0), (-1, 0, 1), (-3, 0, 0), (3, 1, 0), (1, 1, 1), (-2, 0, 1), (-1, 0, 0), (2, 0, 1), (2, 0, 0), (-1, 1, 1), (-3, 1, 0), (2, 1, 0), (2, 1, 1), (-2, 1, 1), (-1, 1, 0), (-2, 1, 0), (-2, 0, 0)),
    1: ((-1, 0, 0), (1, 0, 1), (4, 0, 0), (1, 1, 1), (-1, 1, 1), (1, 1, 0), (-1, 1, 0), (4, 0, 1), (1, 0, 0), (3, 0, 0), (3, 1, 1), (2, 0, 1), (3, 0, 1), (-3, 1, 0), (3, 1, 0), (2, 1, 1), (-2, 0, 1), (2, 0, 0), (-3, 0, 0), (-2, 1, 0), (2, 1, 0), (-1, 0, 1), (-2, 1, 1), (-2, 0, 0)),
    2: ((-1, 1, 0), (1, 0, 1), (4, 0, 0), (-1, 1, 1), (1, 1, 0), (4, 0, 1), (1, 1, 1), (3, 1, 1), (3, 1, 0), (-2, 0, 0), (1, 0, 0), (3, 0, 0), (-3, 1, 0), (-2, 1, 0), (-3, 1, 1), (-2, 0, 1), (3, 0, 1), (-3, 0, 0), (-2, 1, 1), (2, 0, 0), (2, 1, 0), (-1, 0, 0), (-1, 0, 1), (2, 0, 1), (2, 1, 1)),
    3: ((-3, 1, 0), (-1, 1, 0), (4, 0, 0), (-3, 0, 1), (-1, 0, 0), (4, 0, 1), (-3, 1, 1), (-1, 0, 1), (1, 1, 0), (-2, 0, 0), (-1, 1, 1), (3, 1, 0), (1, 0, 0), (3, 0, 0), (1, 1, 1), (-2, 0, 1), (3, 0, 1), (1, 0, 1), (3, 1, 1), (-3, 0, 0), (2, 1, 1), (-2, 1, 0), (2, 1, 0), (2, 0, 1), (-2, 1, 1), (2, 0, 0)),
}
FIRST_SENDS = {
    0: ((3, 1, 0), (1, 0, 0), (-4, 0, 0), (1, 1, 1), (-4, 0, 1), (3, 0, 1), (1, 1, 0), (3, 1, 1)),
    1: ((1, 1, 0), (-1, 0, 0), (-4, 0, 0), (-1, 0, 1), (-3, 1, 1), (-4, 0, 1), (1, 1, 1), (-1, 1, 0), (-1, 1, 1)),
    2: ((1, 1, 0), (1, 0, 0), (1, 0, 1), (-4, 0, 0), (-1, 0, 1), (-1, 1, 1), (1, 1, 1), (-4, 0, 1), (-1, 1, 0), (-1, 0, 0)),
    3: ((-3, 0, 1), (-1, 0, 1), (-4, 0, 0), (-1, 1, 0), (-4, 0, 1), (-3, 0, 0), (-3, 1, 1), (-1, 1, 1), (-3, 1, 0), (-1, 0, 0)),
}
LANES = 4


def size(lane, r, part, node):
    first, end = PARTS[part]
    mine = max(min(NEEDED[r].get(node, 0), end) - first, 0)
    below = [size(lane, r, part, n) for n, parent in TREES[lane, r, part].items() if parent == node]
    return max(below + [mine])


def hops(lane, distance, r, part):
    tree = TREES[(lane + distance) % LANES, r, part]
    return [(node + distance, -node) for node, parent in tree.items() if parent == -distance]


def halves(shape):
    return (lax.broadcasted_iota(jnp.int32, shape, axis) for axis in (0, 1))


def packed(whole):
    whole = whole.astype(jnp.float32)
    upper, lower = whole[:HALF], pltpu.roll(whole[HALF:], HALF, axis=1)
    i, j = halves((HALF, BLK))
    middle = jnp.sum(jnp.where(i == j, lower, 0.0), axis=0, keepdims=True)
    return (
        jnp.where(i > j, lower, upper).astype(jnp.bfloat16),
        jnp.broadcast_to(middle, (PACKED - HALF, BLK)).astype(jnp.bfloat16),
    )


def unpacked(rows, middle):
    rows, middle = rows.astype(jnp.float32), middle.astype(jnp.float32)[:1]
    turned = jnp.concatenate([rows, jnp.zeros_like(rows)], axis=0).T
    i, j = halves((HALF, BLK))
    upper = jnp.where(i <= j, rows, turned[:HALF])
    lower = jnp.where(i > j, rows, jnp.where(i == j, middle, turned[:HALF]))
    lower = jnp.where(j < HALF, turned[HALF:], pltpu.roll(lower, HALF, axis=1))
    return jnp.concatenate([upper, lower], axis=0).astype(jnp.bfloat16)


def band_kernel(device_total, block_total, vals_hbm, cols_hbm, kept_hbm, out, *scratch):
    held = {(m, r): scratch[i * ROWS + r] for i, m in enumerate((0, *OTHERS)) for r in range(ROWS)}
    places = dict(zip((0, *OTHERS), scratch[16:24]))
    left, right, sums, every, vals, cols, kept, middles = scratch[24:32]
    send_sem, recv_sem, psend_sem, precv_sem, fetch_sem = scratch[32:]
    inner = lax.axis_size("col")
    me = lax.axis_index("row") * inner + lax.axis_index("col")

    def device(distance):
        there = lax.rem(me + distance + device_total, device_total)
        return (there // inner, lax.rem(there, inner))

    barrier = pltpu.get_barrier_semaphore()
    for m in (-4, -3, -2, -1, 1, 2, 3, 4):
        pl.semaphore_signal(barrier, inc=1, device_id=device(m), device_id_type=pl.DeviceIdType.MESH)
    fetches = [
        pltpu.make_async_copy(source, target, fetch_sem.at[k])
        for k, (source, target) in enumerate(((cols_hbm, cols), (vals_hbm, vals), (kept_hbm, kept)))
    ]
    for fetch in fetches:
        fetch.start()

    zero = jnp.zeros((BLK, BLK), jnp.bfloat16)
    for m in (0, *OTHERS):
        for r in range(ROWS):
            held[m, r][pl.ds(NONE * UNITS, UNITS)] = zero.reshape(UNITS, UNIT, BLK)
    fetches[0].wait()
    slots = []
    for r in range(ROWS):
        offs = [lax.rem(cols[r, s] - (me * ROWS + r) + block_total, block_total) for s in range(SLOTS)]
        ranks = [
            sum((offs[t] > offs[s]).astype(jnp.int32) for t in range(1, SLOTS) if t != s)
            for s in range(1, SLOTS)
        ]
        slots.append(
            [
                jnp.minimum(
                    sum(s * (ranks[s - 1] == j).astype(jnp.int32) for s in range(1, SLOTS)), SLOTS - 1
                )
                for j in range(SLOTS - 1)
            ]
        )
        places[0][r, 0] = 0
        for o in range(1, REACH + 1):
            place = NONE
            for s in range(1, SLOTS):
                place = jnp.where(offs[s] == o, ranks[s - 1], place)
            places[0][r, o] = place
    fetches[1].wait()
    for r in range(ROWS):
        for j in range(SLOTS - 1):
            held[0, r][pl.ds(j * UNITS, UNITS)] = vals[r, slots[r][j]].reshape(UNITS, UNIT, BLK)
        middle = vals[r, 0]
        middle = (middle.astype(jnp.float32) + middle.T.astype(jnp.float32)).astype(jnp.bfloat16)
        middles[r] = middle
        rows, last = packed(middle)
        held[0, r][pl.ds((SLOTS - 1) * UNITS, UNITS // 2)] = rows.reshape(UNITS // 2, UNIT, BLK)
        held[0, r][(SLOTS - 1) * UNITS + UNITS // 2] = last
    fetches[2].wait()

    pl.semaphore_wait(barrier, 8)

    def remote(lane, m, there, r, part, send, distance):
        blocks = size((lane + m) % LANES, r, part, -there)
        rows = blocks * BLK - (BLK - PACKED if PARTS[part][0] + blocks == SLOTS else 0)
        span = pl.ds(PARTS[part][0] * UNITS, rows // UNIT)
        return pltpu.make_async_remote_copy(
            src_ref=held[m, r].at[span],
            dst_ref=held[there, r].at[span],
            send_sem=send_sem.at[send],
            recv_sem=recv_sem.at[OTHERS.index(there), r, part],
            device_id=device(distance),
            device_id_type=pl.DeviceIdType.MESH,
        )

    def stored(row, offset):
        m, r = row // 2 - 3, row % 2
        first = places[m][r, offset] * UNITS
        return jnp.concatenate([held[m, r][first + k] for k in range(UNITS)], axis=0)

    def block(a, b):
        if a == b:
            m, r = a // 2 - 3, a % 2
            if m == 0:
                return middles[r]
            first = (SLOTS - 1) * UNITS
            rows = held[m, r][pl.ds(first, UNITS // 2)].reshape(HALF, BLK)
            return unpacked(rows, held[m, r][first + UNITS // 2])
        if a < b:
            return stored(a, b - a)
        return stored(b, a - b).T

    def source(a, b):
        row = min(a, b)
        if abs(a - b) > REACH or row > LAST:
            return None
        return (row // 2 - 3, row % 2)

    def traffic(lane):
        sent = []
        here = {(0, 0), (0, 1), None}
        made = set()
        summed = {p: set() for p in range(PAIRS)}
        order = ARRIVALS[lane]
        last_relay = max(i for i, item in enumerate(order) if hops(lane, *item))
        missing = {item: sum(item == (m, r) for m, r, _ in order) for item in {(m, r) for m, r, _ in order}}

        def pass_on(m, r, part, only=None):
            for distance, there in hops(lane, m, r, part):
                if only in (None, distance):
                    copy = remote(lane, m, there, r, part, len(sent), distance)
                    copy.start()
                    sent.append(copy)

        def arrive(m, r, part):
            remote(lane, m, m, r, part, 0, 1).wait_recv()
            missing[m, r] -= 1
            if not missing[m, r]:
                here.add((m, r))

        def place(key, ref, at, a, b):
            if key not in made and source(a, b) in here:
                ref[at] = zero if source(a, b) is None else block(a, b)
                made.add(key)

        def assemble():
            for k in range(LAST + 2):
                for a in range(ROWS):
                    at = (pl.ds(a * BLK, BLK), pl.ds(k * BLK, BLK))
                    place(("left", a, k), left, at, FIRST + a, k)
                for p in range(k // 2 + 1):
                    for c in range(2):
                        at = (p, pl.ds(k * BLK, BLK), pl.ds(c * BLK, BLK))
                        place(("right", p, k, c), right, at, k, FIRST + 1 + 2 * p + c)

        def multiply():
            for p in range(PAIRS):
                ready = [
                    q
                    for q in range(p, PAIRS)
                    if q not in summed[p]
                    and all(("left", a, k) in made for a in range(ROWS) for k in (2 * q, 2 * q + 1))
                    and all(("right", p, k, c) in made for k in (2 * q, 2 * q + 1) for c in range(2))
                ]
                if not ready:
                    continue
                runs = []
                for q in ready:
                    if runs and runs[-1][1] == q:
                        runs[-1][1] = q + 1
                    else:
                        runs.append([q, q + 1])
                total = sums[p] if summed[p] else None
                for low, high in runs:
                    deep = pl.ds(2 * low * BLK, 2 * (high - low) * BLK)
                    part = jnp.dot(left[:, deep], right[p, deep, :], preferred_element_type=jnp.float32)
                    total = part if total is None else total + part
                summed[p].update(ready)
                if len(summed[p]) < PAIRS - p:
                    sums[p] = total
                    continue
                got = total.astype(jnp.bfloat16)
                for a in range(ROWS):
                    for c in range(2):
                        step = 2 * p + c + 1 - a
                        if 1 <= step <= STEPS:
                            every[a, step - 1] = got[a * BLK : (a + 1) * BLK, c * BLK : (c + 1) * BLK]

        for distance, r, part in FIRST_SENDS[lane]:
            pass_on(0, r, part, distance)
        notes = []
        for k, m in enumerate(OTHERS):
            note = pltpu.make_async_remote_copy(
                src_ref=places[0],
                dst_ref=places[m],
                send_sem=psend_sem.at[k],
                recv_sem=precv_sem.at[k],
                device_id=device(-m),
                device_id_type=pl.DeviceIdType.MESH,
            )
            note.start()
            notes.append(note)
        assemble()
        for item in order[: last_relay + 1]:
            arrive(*item)
            pass_on(*item)
        for note in notes:
            note.wait()
        for item in order[last_relay + 1 :]:
            assemble()
            multiply()
            arrive(*item)
        assemble()
        multiply()
        for copy in sent:
            copy.wait_send()

    lane_here = lax.rem(me, LANES)
    for lane in range(LANES):
        pl.when(lane_here == lane)(functools.partial(traffic, lane))
    for a in range(ROWS):
        for t in range(kept.shape[1]):
            step = lax.rem(kept[a, t] - (me * ROWS + a) + block_total, block_total)
            out[a, t] = every[a, jnp.clip(step - 1, 0, STEPS - 1)]


def on_device(upper_vals, upper_cols, result_cols):
    device_total = lax.axis_size("row") * lax.axis_size("col")
    rows, kept_count = result_cols.shape
    places_shape = pltpu.SMEM((ROWS, REACH + 1), jnp.int32)
    most_sent = max(
        len(FIRST_SENDS[lane]) + sum(len(hops(lane, *item)) for item in ARRIVALS[lane]) for lane in range(LANES)
    )

    def kernel(*refs):
        band_kernel(device_total, device_total * ROWS, *refs)

    return pl.pallas_call(
        kernel,
        out_shape=jax.ShapeDtypeStruct((rows, kept_count, BLK, BLK), jnp.bfloat16),
        in_specs=[
            pl.BlockSpec(memory_space=pltpu.HBM),
            pl.BlockSpec(memory_space=pltpu.HBM),
            pl.BlockSpec(memory_space=pltpu.HBM),
        ],
        out_specs=pl.BlockSpec(memory_space=pltpu.VMEM),
        scratch_shapes=[
            *[pltpu.VMEM(((SLOTS + 1) * UNITS, UNIT, BLK), jnp.bfloat16) for _ in range(ROWS * (1 + len(OTHERS)))],
            *[places_shape for _ in range(1 + len(OTHERS))],
            pltpu.VMEM((ROWS * BLK, 2 * PAIRS * BLK), jnp.bfloat16),
            pltpu.VMEM((PAIRS, 2 * PAIRS * BLK, 2 * BLK), jnp.bfloat16),
            pltpu.VMEM((PAIRS, ROWS * BLK, 2 * BLK), jnp.float32),
            pltpu.VMEM((ROWS, STEPS, BLK, BLK), jnp.bfloat16),
            pltpu.VMEM(upper_vals.shape, upper_vals.dtype),
            pltpu.SMEM(upper_cols.shape, upper_cols.dtype),
            pltpu.SMEM(result_cols.shape, result_cols.dtype),
            pltpu.VMEM((ROWS, BLK, BLK), jnp.bfloat16),
            pltpu.SemaphoreType.DMA((most_sent,)),
            pltpu.SemaphoreType.DMA((len(OTHERS), ROWS, 2)),
            pltpu.SemaphoreType.DMA((len(OTHERS),)),
            pltpu.SemaphoreType.DMA((len(OTHERS),)),
            pltpu.SemaphoreType.DMA((3,)),
        ],
        compiler_params=pltpu.CompilerParams(
            collective_id=0, has_side_effects=True, vmem_limit_bytes=40 << 20
        ),
        cost_estimate=pl.CostEstimate(flops=1_200_000_000, bytes_accessed=6_000_000, transcendentals=0),
    )(*(pltpu.with_memory_space_constraint(x, pltpu.HBM) for x in (upper_vals, upper_cols, result_cols)))


def solution(mesh):
    in_specs = (
        P(("row", "col"), None, None, None),
        P(("row", "col"), None),
        P(("row", "col"), None),
    )
    out_specs = P(("row", "col"), None, None, None)
    return jax.shard_map(
        on_device, mesh=mesh, in_specs=in_specs, out_specs=out_specs, check_vma=False
    )
```

```python
import functools

import jax
import jax.numpy as jnp
from jax import lax
from jax.experimental import pallas as pl
from jax.experimental.pallas import tpu as pltpu
from jax.sharding import PartitionSpec as P

BLK = 128
REACH = 7
SLOTS = 6
NONE = SLOTS
ROWS = 2
STEPS = 2 * REACH
FIRST = REACH - 1
LAST = 2 * REACH
PAIRS = REACH + 1
BEHIND = (-3, -2, -1)
AHEAD = (1, 2, 3, 4)
OTHERS = BEHIND + AHEAD
NEEDED = (
    {1: 5, 2: 4, 3: 2, -1: 6, -2: 6, -3: 6, -4: 6},
    {1: 5, 2: 5, 3: 3, -1: 6, -2: 6, -3: 6},
)
PARTS = ((0, 3), (3, 6))
HALF = BLK // 2
PACKED = HALF + 16
UNIT = 16
UNITS = BLK // UNIT
TREES = {
    (0, 0, 0): {-2: -3, -1: -4, 2: 1, -4: 0, 1: 0, -3: -4, 3: 2},
    (0, 0, 1): {-2: -3, 3: 0, 2: 3, 1: -3, -3: -4, -4: 0, -1: -4},
    (0, 1, 0): {1: 0, -3: 1, -1: 3, -2: -3, 2: 3, 3: 0},
    (0, 1, 1): {-2: -1, -1: 3, -3: 1, 2: 3, 3: 0, 1: 0},
    (1, 0, 0): {-4: 0, -3: -4, -2: 2, -1: 0, 1: 2, 3: -1, 2: -1},
    (1, 0, 1): {-4: 0, -1: 0, 1: 2, -2: 2, 2: -1, -3: -4},
    (1, 1, 0): {-3: 1, 2: -1, -2: -3, 3: -1, -1: 0, 1: 0},
    (1, 1, 1): {-3: 1, 1: 0, -2: -3, -1: 0, 2: -1},
    (2, 0, 0): {2: -1, -2: 1, -1: 0, -4: 0, 1: 0, 3: -1, -3: -4},
    (2, 0, 1): {-4: 0, -3: -4, -1: 0, 1: 0, 2: 1, -2: 1},
    (2, 1, 0): {3: -1, -3: 1, -1: 0, 1: 0, -2: 1, 2: 3},
    (2, 1, 1): {1: 0, 3: 0, 2: 3, -2: 1, -3: 1, -1: 0},
    (3, 0, 0): {-4: 0, 1: -3, 3: -1, -3: 0, -1: 0, -2: -1, 2: 1},
    (3, 0, 1): {-2: -1, 1: -3, 2: 1, -3: 0, -4: 0, -1: 0},
    (3, 1, 0): {1: -3, -1: 0, 3: -1, -2: -3, 2: 3, -3: 0},
    (3, 1, 1): {1: -3, -2: -3, 2: -1, -3: 0, -1: 0},
}
ARRIVALS = {
    0: ((1, 0, 0), (4, 0, 0), (3, 0, 0), (1, 0, 1), (3, 0, 1), (4, 0, 1), (1, 1, 0), (3, 1, 0), (-3, 0, 0), (-1, 0, 0), (1, 1, 1), (3, 1, 1), (-1, 0, 1), (-2, 1, 1), (2, 1, 0), (-2, 0, 1), (-3, 1, 0), (2, 0, 1), (-2, 1, 0), (-1, 1, 0), (-2, 0, 0), (2, 1, 1), (-1, 1, 1), (2, 0, 0)),
    1: ((-1, 1, 0), (4, 0, 0), (1, 1, 0), (-1, 0, 0), (4, 0, 1), (1, 0, 1), (-3, 1, 1), (-1, 1, 1), (3, 1, 0), (1, 0, 0), (-3, 1, 0), (3, 0, 0), (1, 1, 1), (3, 0, 1), (3, 1, 1), (2, 0, 0), (2, 1, 0), (-3, 0, 0), (-2, 0, 0), (2, 0, 1), (-2, 1, 1), (-2, 1, 0), (-1, 0, 1), (2, 1, 1), (-2, 0, 1)),
    2: ((-1, 1, 1), (1, 1, 0), (4, 0, 1), (-1, 1, 0), (1, 0, 0), (4, 0, 0), (1, 0, 1), (3, 0, 0), (3, 1, 1), (-3, 1, 0), (1, 1, 1), (-2, 0, 1), (3, 0, 1), (-2, 0, 0), (-3, 0, 0), (3, 1, 0), (-2, 1, 0), (-2, 1, 1), (2, 1, 0), (2, 0, 0), (-1, 0, 0), (2, 0, 1), (2, 1, 1), (-1, 0, 1)),
    3: ((-3, 0, 1), (-1, 1, 0), (4, 0, 0), (-3, 1, 0), (-1, 0, 1), (4, 0, 1), (-3, 1, 1), (-1, 1, 1), (3, 1, 0), (-2, 0, 0), (-1, 0, 0), (1, 0, 0), (1, 1, 0), (3, 0, 1), (1, 1, 1), (-2, 0, 1), (1, 0, 1), (3, 0, 0), (3, 1, 1), (2, 0, 0), (-2, 1, 0), (2, 1, 1), (-3, 0, 0), (-2, 1, 1), (2, 0, 1), (2, 1, 0)),
}
FIRST_SENDS = {
    0: ((1, 1, 0), (3, 0, 1), (-4, 0, 0), (1, 0, 0), (3, 1, 0), (-4, 0, 1), (3, 1, 1), (1, 1, 1)),
    1: ((-4, 0, 0), (-4, 0, 1), (-1, 0, 0), (-1, 0, 1), (-1, 1, 0), (1, 1, 1), (-1, 1, 1), (1, 1, 0)),
    2: ((-1, 1, 0), (-4, 0, 1), (1, 1, 0), (-1, 0, 1), (1, 0, 1), (1, 1, 1), (3, 1, 1), (-1, 0, 0), (-4, 0, 0), (1, 0, 0), (-1, 1, 1)),
    3: ((-4, 0, 0), (-1, 1, 0), (-3, 0, 0), (-1, 0, 0), (-3, 0, 1), (-4, 0, 1), (-1, 0, 1), (-3, 1, 0), (-3, 1, 1), (-1, 1, 1)),
}
LANES = 4


def size(lane, r, part, node):
    first, end = PARTS[part]
    mine = max(min(NEEDED[r].get(node, 0), end) - first, 0)
    below = [size(lane, r, part, n) for n, parent in TREES[lane, r, part].items() if parent == node]
    return max(below + [mine])


def hops(lane, distance, r, part):
    tree = TREES[(lane + distance) % LANES, r, part]
    return [(node + distance, -node) for node, parent in tree.items() if parent == -distance]


def halves(shape):
    return (lax.broadcasted_iota(jnp.int32, shape, axis) for axis in (0, 1))


def packed(whole):
    whole = whole.astype(jnp.float32)
    upper, lower = whole[:HALF], pltpu.roll(whole[HALF:], HALF, axis=1)
    i, j = halves((HALF, BLK))
    middle = jnp.sum(jnp.where(i == j, lower, 0.0), axis=0, keepdims=True)
    return (
        jnp.where(i > j, lower, upper).astype(jnp.bfloat16),
        jnp.broadcast_to(middle, (PACKED - HALF, BLK)).astype(jnp.bfloat16),
    )


def unpacked(rows, middle):
    rows, middle = rows.astype(jnp.float32), middle.astype(jnp.float32)[:1]
    turned = jnp.concatenate([rows, jnp.zeros_like(rows)], axis=0).T
    i, j = halves((HALF, BLK))
    upper = jnp.where(i <= j, rows, turned[:HALF])
    lower = jnp.where(i > j, rows, jnp.where(i == j, middle, turned[:HALF]))
    lower = jnp.where(j < HALF, turned[HALF:], pltpu.roll(lower, HALF, axis=1))
    return jnp.concatenate([upper, lower], axis=0).astype(jnp.bfloat16)


def band_kernel(device_total, block_total, vals_hbm, cols_hbm, kept_hbm, out, *scratch):
    held = {(m, r): scratch[i * ROWS + r] for i, m in enumerate((0, *OTHERS)) for r in range(ROWS)}
    places = dict(zip((0, *OTHERS), scratch[16:24]))
    left, right, sums, every, vals, cols, kept, middles = scratch[24:32]
    send_sem, recv_sem, psend_sem, precv_sem, fetch_sem = scratch[32:]
    inner = lax.axis_size("col")
    me = lax.axis_index("row") * inner + lax.axis_index("col")

    def device(distance):
        there = lax.rem(me + distance + device_total, device_total)
        return (there // inner, lax.rem(there, inner))

    barrier = pltpu.get_barrier_semaphore()
    for m in (-4, -3, -2, -1, 1, 2, 3, 4):
        pl.semaphore_signal(barrier, inc=1, device_id=device(m), device_id_type=pl.DeviceIdType.MESH)
    fetches = [
        pltpu.make_async_copy(source, target, fetch_sem.at[k])
        for k, (source, target) in enumerate(((cols_hbm, cols), (vals_hbm, vals), (kept_hbm, kept)))
    ]
    for fetch in fetches:
        fetch.start()

    zero = jnp.zeros((BLK, BLK), jnp.bfloat16)
    for m in (0, *OTHERS):
        for r in range(ROWS):
            held[m, r][pl.ds(NONE * UNITS, UNITS)] = zero.reshape(UNITS, UNIT, BLK)
    fetches[0].wait()
    slots = []
    for r in range(ROWS):
        offs = [lax.rem(cols[r, s] - (me * ROWS + r) + block_total, block_total) for s in range(SLOTS)]
        ranks = [
            sum((offs[t] > offs[s]).astype(jnp.int32) for t in range(1, SLOTS) if t != s)
            for s in range(1, SLOTS)
        ]
        slots.append(
            [
                jnp.minimum(
                    sum(s * (ranks[s - 1] == j).astype(jnp.int32) for s in range(1, SLOTS)), SLOTS - 1
                )
                for j in range(SLOTS - 1)
            ]
        )
        places[0][r, 0] = 0
        for o in range(1, REACH + 1):
            place = NONE
            for s in range(1, SLOTS):
                place = jnp.where(offs[s] == o, ranks[s - 1], place)
            places[0][r, o] = place
    fetches[1].wait()
    for r in range(ROWS):
        for j in range(SLOTS - 1):
            held[0, r][pl.ds(j * UNITS, UNITS)] = vals[r, slots[r][j]].reshape(UNITS, UNIT, BLK)
        middle = vals[r, 0]
        middle = (middle.astype(jnp.float32) + middle.T.astype(jnp.float32)).astype(jnp.bfloat16)
        middles[r] = middle
        rows, last = packed(middle)
        held[0, r][pl.ds((SLOTS - 1) * UNITS, UNITS // 2)] = rows.reshape(UNITS // 2, UNIT, BLK)
        held[0, r][(SLOTS - 1) * UNITS + UNITS // 2] = last
    fetches[2].wait()

    pl.semaphore_wait(barrier, 8)

    def remote(lane, m, there, r, part, send, distance):
        blocks = size((lane + m) % LANES, r, part, -there)
        rows = blocks * BLK - (BLK - PACKED if PARTS[part][0] + blocks == SLOTS else 0)
        span = pl.ds(PARTS[part][0] * UNITS, rows // UNIT)
        return pltpu.make_async_remote_copy(
            src_ref=held[m, r].at[span],
            dst_ref=held[there, r].at[span],
            send_sem=send_sem.at[send],
            recv_sem=recv_sem.at[OTHERS.index(there), r, part],
            device_id=device(distance),
            device_id_type=pl.DeviceIdType.MESH,
        )

    def stored(row, offset):
        m, r = row // 2 - 3, row % 2
        first = places[m][r, offset] * UNITS
        return jnp.concatenate([held[m, r][first + k] for k in range(UNITS)], axis=0)

    def block(a, b):
        if a == b:
            m, r = a // 2 - 3, a % 2
            if m == 0:
                return middles[r]
            first = (SLOTS - 1) * UNITS
            rows = held[m, r][pl.ds(first, UNITS // 2)].reshape(HALF, BLK)
            return unpacked(rows, held[m, r][first + UNITS // 2])
        if a < b:
            return stored(a, b - a)
        return stored(b, a - b).T

    def source(a, b):
        row = min(a, b)
        if abs(a - b) > REACH or row > LAST:
            return None
        return (row // 2 - 3, row % 2)

    def traffic(lane):
        sent = []
        here = {(0, 0), (0, 1), None}
        made = set()
        summed = {p: set() for p in range(PAIRS)}
        order = ARRIVALS[lane]
        last_relay = max(i for i, item in enumerate(order) if hops(lane, *item))
        missing = {item: sum(item == (m, r) for m, r, _ in order) for item in {(m, r) for m, r, _ in order}}

        def pass_on(m, r, part, only=None):
            for distance, there in hops(lane, m, r, part):
                if only in (None, distance):
                    copy = remote(lane, m, there, r, part, len(sent), distance)
                    copy.start()
                    sent.append(copy)

        def arrive(m, r, part):
            remote(lane, m, m, r, part, 0, 1).wait_recv()
            missing[m, r] -= 1
            if not missing[m, r]:
                here.add((m, r))

        def place(key, ref, at, a, b):
            if key not in made and source(a, b) in here:
                ref[at] = zero if source(a, b) is None else block(a, b)
                made.add(key)

        def assemble():
            for k in range(LAST + 2):
                for a in range(ROWS):
                    at = (pl.ds(a * BLK, BLK), pl.ds(k * BLK, BLK))
                    place(("left", a, k), left, at, FIRST + a, k)
                for p in range(k // 2 + 1):
                    for c in range(2):
                        at = (p, pl.ds(k * BLK, BLK), pl.ds(c * BLK, BLK))
                        place(("right", p, k, c), right, at, k, FIRST + 1 + 2 * p + c)

        def multiply():
            for p in range(PAIRS):
                ready = [
                    q
                    for q in range(p, PAIRS)
                    if q not in summed[p]
                    and all(("left", a, k) in made for a in range(ROWS) for k in (2 * q, 2 * q + 1))
                    and all(("right", p, k, c) in made for k in (2 * q, 2 * q + 1) for c in range(2))
                ]
                if not ready:
                    continue
                runs = []
                for q in ready:
                    if runs and runs[-1][1] == q:
                        runs[-1][1] = q + 1
                    else:
                        runs.append([q, q + 1])
                total = sums[p] if summed[p] else None
                for low, high in runs:
                    deep = pl.ds(2 * low * BLK, 2 * (high - low) * BLK)
                    part = jnp.dot(left[:, deep], right[p, deep, :], preferred_element_type=jnp.float32)
                    total = part if total is None else total + part
                summed[p].update(ready)
                if len(summed[p]) < PAIRS - p:
                    sums[p] = total
                    continue
                got = total.astype(jnp.bfloat16)
                for a in range(ROWS):
                    for c in range(2):
                        step = 2 * p + c + 1 - a
                        if 1 <= step <= STEPS:
                            every[a, step - 1] = got[a * BLK : (a + 1) * BLK, c * BLK : (c + 1) * BLK]

        for distance, r, part in FIRST_SENDS[lane]:
            pass_on(0, r, part, distance)
        notes = []
        for k, m in enumerate(OTHERS):
            note = pltpu.make_async_remote_copy(
                src_ref=places[0],
                dst_ref=places[m],
                send_sem=psend_sem.at[k],
                recv_sem=precv_sem.at[k],
                device_id=device(-m),
                device_id_type=pl.DeviceIdType.MESH,
            )
            note.start()
            notes.append(note)
        assemble()
        for item in order[: last_relay + 1]:
            arrive(*item)
            pass_on(*item)
        for note in notes:
            note.wait()
        for item in order[last_relay + 1 :]:
            assemble()
            multiply()
            arrive(*item)
        assemble()
        multiply()
        for copy in sent:
            copy.wait_send()

    lane_here = lax.rem(me, LANES)
    for lane in range(LANES):
        pl.when(lane_here == lane)(functools.partial(traffic, lane))
    for a in range(ROWS):
        for t in range(kept.shape[1]):
            step = lax.rem(kept[a, t] - (me * ROWS + a) + block_total, block_total)
            out[a, t] = every[a, jnp.clip(step - 1, 0, STEPS - 1)]


def on_device(upper_vals, upper_cols, result_cols):
    device_total = lax.axis_size("row") * lax.axis_size("col")
    rows, kept_count = result_cols.shape
    places_shape = pltpu.SMEM((ROWS, REACH + 1), jnp.int32)
    most_sent = max(
        len(FIRST_SENDS[lane]) + sum(len(hops(lane, *item)) for item in ARRIVALS[lane]) for lane in range(LANES)
    )

    def kernel(*refs):
        band_kernel(device_total, device_total * ROWS, *refs)

    return pl.pallas_call(
        kernel,
        out_shape=jax.ShapeDtypeStruct((rows, kept_count, BLK, BLK), jnp.bfloat16),
        in_specs=[
            pl.BlockSpec(memory_space=pltpu.HBM),
            pl.BlockSpec(memory_space=pltpu.HBM),
            pl.BlockSpec(memory_space=pltpu.HBM),
        ],
        out_specs=pl.BlockSpec(memory_space=pltpu.VMEM),
        scratch_shapes=[
            *[pltpu.VMEM(((SLOTS + 1) * UNITS, UNIT, BLK), jnp.bfloat16) for _ in range(ROWS * (1 + len(OTHERS)))],
            *[places_shape for _ in range(1 + len(OTHERS))],
            pltpu.VMEM((ROWS * BLK, 2 * PAIRS * BLK), jnp.bfloat16),
            pltpu.VMEM((PAIRS, 2 * PAIRS * BLK, 2 * BLK), jnp.bfloat16),
            pltpu.VMEM((PAIRS, ROWS * BLK, 2 * BLK), jnp.float32),
            pltpu.VMEM((ROWS, STEPS, BLK, BLK), jnp.bfloat16),
            pltpu.VMEM(upper_vals.shape, upper_vals.dtype),
            pltpu.SMEM(upper_cols.shape, upper_cols.dtype),
            pltpu.SMEM(result_cols.shape, result_cols.dtype),
            pltpu.VMEM((ROWS, BLK, BLK), jnp.bfloat16),
            pltpu.SemaphoreType.DMA((most_sent,)),
            pltpu.SemaphoreType.DMA((len(OTHERS), ROWS, 2)),
            pltpu.SemaphoreType.DMA((len(OTHERS),)),
            pltpu.SemaphoreType.DMA((len(OTHERS),)),
            pltpu.SemaphoreType.DMA((3,)),
        ],
        compiler_params=pltpu.CompilerParams(
            collective_id=0, has_side_effects=True, vmem_limit_bytes=40 << 20
        ),
        cost_estimate=pl.CostEstimate(flops=1_200_000_000, bytes_accessed=6_000_000, transcendentals=0),
    )(*(pltpu.with_memory_space_constraint(x, pltpu.HBM) for x in (upper_vals, upper_cols, result_cols)))


def solution(mesh):
    in_specs = (
        P(("row", "col"), None, None, None),
        P(("row", "col"), None),
        P(("row", "col"), None),
    )
    out_specs = P(("row", "col"), None, None, None)
    return jax.shard_map(
        on_device, mesh=mesh, in_specs=in_specs, out_specs=out_specs, check_vma=False
    )
```

```python
import functools

import jax
import jax.numpy as jnp
from jax import lax
from jax.experimental import pallas as pl
from jax.experimental.pallas import tpu as pltpu
from jax.sharding import PartitionSpec as P

BLK = 128
REACH = 7
SLOTS = 6
NONE = SLOTS
ROWS = 2
STEPS = 2 * REACH
FIRST = REACH - 1
LAST = 2 * REACH
PAIRS = REACH + 1
BEHIND = (-3, -2, -1)
AHEAD = (1, 2, 3, 4)
OTHERS = BEHIND + AHEAD
NEEDED = (
    {1: 5, 2: 4, 3: 2, -1: 6, -2: 6, -3: 6, -4: 6},
    {1: 5, 2: 5, 3: 3, -1: 6, -2: 6, -3: 6},
)
PARTS = ((0, 3), (3, 6))
HALF = BLK // 2
PACKED = HALF + 16
UNIT = 16
UNITS = BLK // UNIT
TREES = {
    (0, 0, 0): {-2: -3, -1: -4, 2: 1, -4: 0, 1: 0, -3: -4, 3: 2},
    (0, 0, 1): {-2: -3, 3: 0, 2: 3, 1: -3, -3: -4, -4: 0, -1: -4},
    (0, 1, 0): {1: 0, -3: 1, -1: 3, -2: -3, 2: 3, 3: 0},
    (0, 1, 1): {-2: -1, -1: 3, -3: 1, 2: 3, 3: 0, 1: 0},
    (1, 0, 0): {-4: 0, -3: -4, -2: 2, -1: 0, 1: 2, 3: -1, 2: -1},
    (1, 0, 1): {-4: 0, -1: 0, 1: 2, -2: 2, 2: -1, -3: -4},
    (1, 1, 0): {-3: 1, 2: -1, -2: -3, 3: -1, -1: 0, 1: 0},
    (1, 1, 1): {-3: 1, 1: 0, -2: -3, -1: 0, 2: -1},
    (2, 0, 0): {2: -1, -2: 1, -1: 0, -4: 0, 1: 0, 3: -1, -3: -4},
    (2, 0, 1): {-4: 0, -3: -4, -1: 0, 1: 0, 2: 1, -2: 1},
    (2, 1, 0): {3: -1, -3: 1, -1: 0, 1: 0, -2: 1, 2: 3},
    (2, 1, 1): {1: 0, 3: 0, 2: 3, -2: 1, -3: 1, -1: 0},
    (3, 0, 0): {-4: 0, 1: -3, 3: -1, -3: 0, -1: 0, -2: -1, 2: 1},
    (3, 0, 1): {-2: -1, 1: -3, 2: 1, -3: 0, -4: 0, -1: 0},
    (3, 1, 0): {1: -3, -1: 0, 3: -1, -2: -3, 2: 3, -3: 0},
    (3, 1, 1): {1: -3, -2: -3, 2: -1, -3: 0, -1: 0},
}
ARRIVALS = {
    0: ((1, 0, 0), (4, 0, 0), (3, 0, 0), (1, 0, 1), (3, 0, 1), (4, 0, 1), (1, 1, 0), (3, 1, 0), (-3, 0, 0), (-1, 0, 0), (1, 1, 1), (3, 1, 1), (-1, 0, 1), (-2, 1, 1), (2, 1, 0), (-2, 0, 1), (-3, 1, 0), (2, 0, 1), (-2, 1, 0), (-1, 1, 0), (-2, 0, 0), (2, 1, 1), (-1, 1, 1), (2, 0, 0)),
    1: ((-1, 1, 0), (4, 0, 0), (1, 1, 0), (-1, 0, 0), (4, 0, 1), (1, 0, 1), (-3, 1, 1), (-1, 1, 1), (3, 1, 0), (1, 0, 0), (-3, 1, 0), (3, 0, 0), (1, 1, 1), (3, 0, 1), (3, 1, 1), (2, 0, 0), (2, 1, 0), (-3, 0, 0), (-2, 0, 0), (2, 0, 1), (-2, 1, 1), (-2, 1, 0), (-1, 0, 1), (2, 1, 1), (-2, 0, 1)),
    2: ((-1, 1, 1), (1, 1, 0), (4, 0, 1), (-1, 1, 0), (1, 0, 0), (4, 0, 0), (1, 0, 1), (3, 0, 0), (3, 1, 1), (-3, 1, 0), (1, 1, 1), (-2, 0, 1), (3, 0, 1), (-2, 0, 0), (-3, 0, 0), (3, 1, 0), (-2, 1, 0), (-2, 1, 1), (2, 1, 0), (2, 0, 0), (-1, 0, 0), (2, 0, 1), (2, 1, 1), (-1, 0, 1)),
    3: ((-3, 0, 1), (-1, 1, 0), (4, 0, 0), (-3, 1, 0), (-1, 0, 1), (4, 0, 1), (-3, 1, 1), (-1, 1, 1), (3, 1, 0), (-2, 0, 0), (-1, 0, 0), (1, 0, 0), (1, 1, 0), (3, 0, 1), (1, 1, 1), (-2, 0, 1), (1, 0, 1), (3, 0, 0), (3, 1, 1), (2, 0, 0), (-2, 1, 0), (2, 1, 1), (-3, 0, 0), (-2, 1, 1), (2, 0, 1), (2, 1, 0)),
}
FIRST_SENDS = {
    0: ((1, 1, 0), (3, 0, 1), (-4, 0, 0), (1, 0, 0), (3, 1, 0), (-4, 0, 1), (3, 1, 1), (1, 1, 1)),
    1: ((-4, 0, 0), (-4, 0, 1), (-1, 0, 0), (-1, 0, 1), (-1, 1, 0), (1, 1, 1), (-1, 1, 1), (1, 1, 0)),
    2: ((-1, 1, 0), (-4, 0, 1), (1, 1, 0), (-1, 0, 1), (1, 0, 1), (1, 1, 1), (3, 1, 1), (-1, 0, 0), (-4, 0, 0), (1, 0, 0), (-1, 1, 1)),
    3: ((-4, 0, 0), (-1, 1, 0), (-3, 0, 0), (-1, 0, 0), (-3, 0, 1), (-4, 0, 1), (-1, 0, 1), (-3, 1, 0), (-3, 1, 1), (-1, 1, 1)),
}
LANES = 4


def size(lane, r, part, node):
    first, end = PARTS[part]
    mine = max(min(NEEDED[r].get(node, 0), end) - first, 0)
    below = [size(lane, r, part, n) for n, parent in TREES[lane, r, part].items() if parent == node]
    return max(below + [mine])


def hops(lane, distance, r, part):
    tree = TREES[(lane + distance) % LANES, r, part]
    return [(node + distance, -node) for node, parent in tree.items() if parent == -distance]


def halves(shape):
    return (lax.broadcasted_iota(jnp.int32, shape, axis) for axis in (0, 1))


def packed(whole):
    whole = whole.astype(jnp.float32)
    upper, lower = whole[:HALF], pltpu.roll(whole[HALF:], HALF, axis=1)
    i, j = halves((HALF, BLK))
    middle = jnp.sum(jnp.where(i == j, lower, 0.0), axis=0, keepdims=True)
    return (
        jnp.where(i > j, lower, upper).astype(jnp.bfloat16),
        jnp.broadcast_to(middle, (PACKED - HALF, BLK)).astype(jnp.bfloat16),
    )


def unpacked(rows, middle):
    rows, middle = rows.astype(jnp.float32), middle.astype(jnp.float32)[:1]
    turned = jnp.concatenate([rows, jnp.zeros_like(rows)], axis=0).T
    i, j = halves((HALF, BLK))
    upper = jnp.where(i <= j, rows, turned[:HALF])
    lower = jnp.where(i > j, rows, jnp.where(i == j, middle, turned[:HALF]))
    lower = jnp.where(j < HALF, turned[HALF:], pltpu.roll(lower, HALF, axis=1))
    return jnp.concatenate([upper, lower], axis=0).astype(jnp.bfloat16)


def band_kernel(device_total, block_total, vals_hbm, cols_hbm, kept_hbm, out, *scratch):
    held = {(m, r): scratch[i * ROWS + r] for i, m in enumerate((0, *OTHERS)) for r in range(ROWS)}
    places = dict(zip((0, *OTHERS), scratch[16:24]))
    left, right, sums, every, vals, cols, kept, middles = scratch[24:32]
    send_sem, recv_sem, psend_sem, precv_sem, fetch_sem = scratch[32:]
    inner = lax.axis_size("col")
    me = lax.axis_index("row") * inner + lax.axis_index("col")

    def device(distance):
        there = lax.rem(me + distance + device_total, device_total)
        return (there // inner, lax.rem(there, inner))

    barrier = pltpu.get_barrier_semaphore()
    for m in (-4, -3, -2, -1, 1, 2, 3, 4):
        pl.semaphore_signal(barrier, inc=1, device_id=device(m), device_id_type=pl.DeviceIdType.MESH)
    fetches = [
        pltpu.make_async_copy(source, target, fetch_sem.at[k])
        for k, (source, target) in enumerate(((cols_hbm, cols), (vals_hbm, vals), (kept_hbm, kept)))
    ]
    for fetch in fetches:
        fetch.start()

    zero = jnp.zeros((BLK, BLK), jnp.bfloat16)
    for m in (0, *OTHERS):
        for r in range(ROWS):
            held[m, r][pl.ds(NONE * UNITS, UNITS)] = zero.reshape(UNITS, UNIT, BLK)
    fetches[0].wait()
    slots = []
    for r in range(ROWS):
        offs = [lax.rem(cols[r, s] - (me * ROWS + r) + block_total, block_total) for s in range(SLOTS)]
        ranks = [
            sum((offs[t] > offs[s]).astype(jnp.int32) for t in range(1, SLOTS) if t != s)
            for s in range(1, SLOTS)
        ]
        slots.append(
            [
                jnp.minimum(
                    sum(s * (ranks[s - 1] == j).astype(jnp.int32) for s in range(1, SLOTS)), SLOTS - 1
                )
                for j in range(SLOTS - 1)
            ]
        )
        places[0][r, 0] = 0
        for o in range(1, REACH + 1):
            place = NONE
            for s in range(1, SLOTS):
                place = jnp.where(offs[s] == o, ranks[s - 1], place)
            places[0][r, o] = place
    fetches[1].wait()
    for r in range(ROWS):
        for j in range(SLOTS - 1):
            held[0, r][pl.ds(j * UNITS, UNITS)] = vals[r, slots[r][j]].reshape(UNITS, UNIT, BLK)
        middle = vals[r, 0]
        middle = (middle.astype(jnp.float32) + middle.T.astype(jnp.float32)).astype(jnp.bfloat16)
        middles[r] = middle
        rows, last = packed(middle)
        held[0, r][pl.ds((SLOTS - 1) * UNITS, UNITS // 2)] = rows.reshape(UNITS // 2, UNIT, BLK)
        held[0, r][(SLOTS - 1) * UNITS + UNITS // 2] = last
    fetches[2].wait()

    pl.semaphore_wait(barrier, 8)

    def remote(lane, m, there, r, part, send, distance):
        blocks = size((lane + m) % LANES, r, part, -there)
        rows = blocks * BLK - (BLK - PACKED if PARTS[part][0] + blocks == SLOTS else 0)
        span = pl.ds(PARTS[part][0] * UNITS, rows // UNIT)
        return pltpu.make_async_remote_copy(
            src_ref=held[m, r].at[span],
            dst_ref=held[there, r].at[span],
            send_sem=send_sem.at[send],
            recv_sem=recv_sem.at[OTHERS.index(there), r, part],
            device_id=device(distance),
            device_id_type=pl.DeviceIdType.MESH,
        )

    def stored(row, offset):
        m, r = row // 2 - 3, row % 2
        first = places[m][r, offset] * UNITS
        return jnp.concatenate([held[m, r][first + k] for k in range(UNITS)], axis=0)

    def block(a, b):
        if a == b:
            m, r = a // 2 - 3, a % 2
            if m == 0:
                return middles[r]
            first = (SLOTS - 1) * UNITS
            rows = held[m, r][pl.ds(first, UNITS // 2)].reshape(HALF, BLK)
            return unpacked(rows, held[m, r][first + UNITS // 2])
        if a < b:
            return stored(a, b - a)
        return stored(b, a - b).T

    def source(a, b):
        row = min(a, b)
        if abs(a - b) > REACH or row > LAST:
            return None
        return (row // 2 - 3, row % 2)

    def traffic(lane):
        sent = []
        here = {(0, 0), (0, 1), None}
        made = set()
        summed = {p: set() for p in range(PAIRS)}
        order = ARRIVALS[lane]
        last_relay = max(i for i, item in enumerate(order) if hops(lane, *item))
        missing = {item: sum(item == (m, r) for m, r, _ in order) for item in {(m, r) for m, r, _ in order}}

        def pass_on(m, r, part, only=None):
            for distance, there in hops(lane, m, r, part):
                if only in (None, distance):
                    copy = remote(lane, m, there, r, part, len(sent), distance)
                    copy.start()
                    sent.append(copy)

        def arrive(m, r, part):
            remote(lane, m, m, r, part, 0, 1).wait_recv()
            missing[m, r] -= 1
            if not missing[m, r]:
                here.add((m, r))

        def place(key, ref, at, a, b):
            if key not in made and source(a, b) in here:
                ref[at] = zero if source(a, b) is None else block(a, b)
                made.add(key)

        def assemble():
            for k in range(LAST + 2):
                for a in range(ROWS):
                    at = (pl.ds(a * BLK, BLK), pl.ds(k * BLK, BLK))
                    place(("left", a, k), left, at, FIRST + a, k)
                for p in range(k // 2 + 1):
                    for c in range(2):
                        at = (p, pl.ds(k * BLK, BLK), pl.ds(c * BLK, BLK))
                        place(("right", p, k, c), right, at, k, FIRST + 1 + 2 * p + c)

        def multiply():
            for p in range(PAIRS):
                ready = [
                    q
                    for q in range(p, PAIRS)
                    if q not in summed[p]
                    and all(("left", a, k) in made for a in range(ROWS) for k in (2 * q, 2 * q + 1))
                    and all(("right", p, k, c) in made for k in (2 * q, 2 * q + 1) for c in range(2))
                ]
                if not ready:
                    continue
                runs = []
                for q in ready:
                    if runs and runs[-1][1] == q:
                        runs[-1][1] = q + 1
                    else:
                        runs.append([q, q + 1])
                total = sums[p] if summed[p] else None
                for low, high in runs:
                    deep = pl.ds(2 * low * BLK, 2 * (high - low) * BLK)
                    part = jnp.dot(left[:, deep], right[p, deep, :], preferred_element_type=jnp.float32)
                    total = part if total is None else total + part
                summed[p].update(ready)
                if len(summed[p]) < PAIRS - p:
                    sums[p] = total
                    continue
                got = total.astype(jnp.bfloat16)
                for a in range(ROWS):
                    for c in range(2):
                        step = 2 * p + c + 1 - a
                        if 1 <= step <= STEPS:
                            every[a, step - 1] = got[a * BLK : (a + 1) * BLK, c * BLK : (c + 1) * BLK]

        for distance, r, part in FIRST_SENDS[lane]:
            pass_on(0, r, part, distance)
        notes = []
        for k, m in enumerate(OTHERS):
            note = pltpu.make_async_remote_copy(
                src_ref=places[0],
                dst_ref=places[m],
                send_sem=psend_sem.at[k],
                recv_sem=precv_sem.at[k],
                device_id=device(-m),
                device_id_type=pl.DeviceIdType.MESH,
            )
            note.start()
            notes.append(note)
        assemble()
        for item in order[: last_relay + 1]:
            arrive(*item)
            pass_on(*item)
        for note in notes:
            note.wait()
        for item in order[last_relay + 1 :]:
            assemble()
            multiply()
            arrive(*item)
        assemble()
        multiply()
        for a in range(ROWS):
            for t in range(kept.shape[1]):
                step = lax.rem(kept[a, t] - (me * ROWS + a) + block_total, block_total)
                out[a, t] = every[a, jnp.clip(step - 1, 0, STEPS - 1)]
        for copy in sent:
            copy.wait_send()

    lane_here = lax.rem(me, LANES)
    for lane in range(LANES):
        pl.when(lane_here == lane)(functools.partial(traffic, lane))


def on_device(upper_vals, upper_cols, result_cols):
    device_total = lax.axis_size("row") * lax.axis_size("col")
    rows, kept_count = result_cols.shape
    places_shape = pltpu.SMEM((ROWS, REACH + 1), jnp.int32)
    most_sent = max(
        len(FIRST_SENDS[lane]) + sum(len(hops(lane, *item)) for item in ARRIVALS[lane]) for lane in range(LANES)
    )

    def kernel(*refs):
        band_kernel(device_total, device_total * ROWS, *refs)

    return pl.pallas_call(
        kernel,
        out_shape=jax.ShapeDtypeStruct((rows, kept_count, BLK, BLK), jnp.bfloat16),
        in_specs=[
            pl.BlockSpec(memory_space=pltpu.HBM),
            pl.BlockSpec(memory_space=pltpu.HBM),
            pl.BlockSpec(memory_space=pltpu.HBM),
        ],
        out_specs=pl.BlockSpec(memory_space=pltpu.VMEM),
        scratch_shapes=[
            *[pltpu.VMEM(((SLOTS + 1) * UNITS, UNIT, BLK), jnp.bfloat16) for _ in range(ROWS * (1 + len(OTHERS)))],
            *[places_shape for _ in range(1 + len(OTHERS))],
            pltpu.VMEM((ROWS * BLK, 2 * PAIRS * BLK), jnp.bfloat16),
            pltpu.VMEM((PAIRS, 2 * PAIRS * BLK, 2 * BLK), jnp.bfloat16),
            pltpu.VMEM((PAIRS, ROWS * BLK, 2 * BLK), jnp.float32),
            pltpu.VMEM((ROWS, STEPS, BLK, BLK), jnp.bfloat16),
            pltpu.VMEM(upper_vals.shape, upper_vals.dtype),
            pltpu.SMEM(upper_cols.shape, upper_cols.dtype),
            pltpu.SMEM(result_cols.shape, result_cols.dtype),
            pltpu.VMEM((ROWS, BLK, BLK), jnp.bfloat16),
            pltpu.SemaphoreType.DMA((most_sent,)),
            pltpu.SemaphoreType.DMA((len(OTHERS), ROWS, 2)),
            pltpu.SemaphoreType.DMA((len(OTHERS),)),
            pltpu.SemaphoreType.DMA((len(OTHERS),)),
            pltpu.SemaphoreType.DMA((3,)),
        ],
        compiler_params=pltpu.CompilerParams(
            collective_id=0, has_side_effects=True, vmem_limit_bytes=40 << 20
        ),
        cost_estimate=pl.CostEstimate(flops=1_200_000_000, bytes_accessed=6_000_000, transcendentals=0),
    )(*(pltpu.with_memory_space_constraint(x, pltpu.HBM) for x in (upper_vals, upper_cols, result_cols)))


def solution(mesh):
    in_specs = (
        P(("row", "col"), None, None, None),
        P(("row", "col"), None),
        P(("row", "col"), None),
    )
    out_specs = P(("row", "col"), None, None, None)
    return jax.shard_map(
        on_device, mesh=mesh, in_specs=in_specs, out_specs=out_specs, check_vma=False
    )
```
